768 devices in a mesh: pair: 48 (over x, z), orb: 16 (over y, core).
Axes of the slice: x: 4, y: 8, z: 12, core: 2. Of those that a mesh axis runs over, the one named last changes fastest.
Arguments:
- amplitudes: float32 [144, 64, 64, 640], P('pair', None, 'orb'), may hold values from -3 to 3
- integrals: float32 [640, 64, 768], P('orb', None, 'pair'), may hold values from -0.03125 to 0.03125
- a_irrep: int32 [144], P('pair'), may hold values from 0 to 7
- b_irrep: int32 [12], replicated, may hold values from 0 to 7
- occ_irrep: int32 [64], replicated, may hold values from 0 to 7
Outputs:
- cycle_residual: float32 [144, 64, 768], P('pair', 'orb')
The draws below stay inside these ranges and needn't reach their ends.
All inputs are finite; a program needn't handle non-finite values.
Results may differ from the reference program's by a relative error of at most 0.000082.
Values sent between devices are 32-bit elements; how exact they have to be, the bound alone decides.
No kernel may reach another device: no remote copies, remote signals or barrier semaphores. Data moves between devices by JAX's collectives and lax.ppermute only.
A program may use at most 64 MiB of HBM per device.

```python
import jax
import jax.numpy as jnp
from jax import lax

O = 64
V = 640
BW = 12
AW = 144
COLS = 768


def place_ends(result, stream_key, low, top_value):
    longest = result.shape.index(max(result.shape))
    spots = []
    for shift in (0, 1):
        where = [jax.random.randint(jax.random.fold_in(stream_key, axis), (), 0, length) for axis, length in enumerate(result.shape)]
        where[longest] = (where[longest] + shift) % result.shape[longest]
        spots.append(tuple(where))
    return result.at[spots[0]].set(low).at[spots[1]].set(top_value)


def steps_of(key, dims, split, low, largest):
    def one(dim, parts):
        steps = jax.random.uniform(jax.random.fold_in(jax.random.fold_in(key, 6), dim), (parts,), jnp.float32, low / len(split), largest / len(split))
        return jnp.repeat(jnp.exp(steps), dims[dim] // parts).reshape((-1,) + (1,) * (len(dims) - dim - 1))

    loudness = one(*split[0])
    for cut in split[1:]:
        loudness = loudness * one(*cut)
    return loudness


def gaussian(own_key, shape, deviation, limit, split=(), dtype=jnp.bfloat16):
    drawn = deviation * jax.random.normal(own_key, shape, jnp.float32)
    if split:
        drawn = drawn * steps_of(own_key, shape, split, -0.22, 0.18)
    return jnp.clip(drawn, -limit, limit).astype(dtype)


def setup_inputs(seed: int = 0) -> dict:
    key_of = jax.random.split(jax.random.key(seed), 6)
    return {
        "amplitudes": gaussian(key_of[0], (AW, O, O, V), 0.5, 3.0, ((0, 48), (2, 16)), jnp.float32),
        "integrals": gaussian(key_of[1], (V, O, COLS), (V * O) ** -0.5, 0.03125, ((0, 16), (2, 48)), jnp.float32),
        "a_irrep": place_ends(jax.random.randint(key_of[2], (AW,), 0, 8), jax.random.fold_in(key_of[2], 1), 0, 7).astype(jnp.int32),
        "b_irrep": place_ends(jax.random.randint(key_of[3], (BW,), 0, 8), jax.random.fold_in(key_of[3], 1), 0, 7).astype(jnp.int32),
        "occ_irrep": place_ends(jax.random.randint(key_of[4], (O,), 0, 8), jax.random.fold_in(key_of[4], 1), 0, 7).astype(jnp.int32),
    }


def reference(amplitudes, integrals, a_irrep, b_irrep, occ_irrep):
    flat_integrals = jnp.transpose(integrals, (1, 0, 2)).reshape(O * V, BW * O)

    def one_orbital(block):
        spin = 2.0 * block - jnp.transpose(block, (1, 0, 2))
        return jnp.dot(spin.reshape(O, O * V), flat_integrals, precision=lax.Precision.HIGHEST, preferred_element_type=jnp.float32)

    cycle = lax.map(one_orbital, amplitudes)
    col_sym = jnp.bitwise_xor(b_irrep[:, None], occ_irrep[None, :]).reshape(BW * O)
    symmetry = jnp.bitwise_xor(jnp.bitwise_xor(a_irrep[:, None, None], occ_irrep[None, :, None]), col_sym[None, None, :])
    return jnp.where(symmetry == 0, cycle, jnp.float32(0.0))
```

```python
import jax
import jax.numpy as jnp
from jax import lax
from jax.experimental import pallas as pl
from jax.experimental.pallas import tpu as pltpu
from jax.sharding import Mesh, PartitionSpec as P

MIB = 1 << 20


def spin_kernel(xl_ref, own_ref, other_ref, swapped_ref, high_ref, low_ref, rows):
    xl = xl_ref[0]
    _, window, occupied, virtual = own_ref.shape
    for rel, direct in enumerate((own_ref, other_ref)):
        source = xl if rel == 0 else 1 - xl
        for j in range(2):
            for a in range(window):
                for orb in range(occupied // 4):
                    rows[pl.ds(4 * orb, 4), :] = swapped_ref[2 * orb + source, j, a]
                spin = 2.0 * direct[j, a] - rows[...]
                high = spin.astype(jnp.bfloat16)
                low = (spin - high.astype(jnp.float32)).astype(jnp.bfloat16)
                at = (pl.ds((rel * window + a) * occupied, occupied), pl.ds(j * virtual, virtual))
                high_ref[at] = high
                low_ref[at] = low


def spin_rows(xl, own, other, swapped):
    _, window, occupied, virtual = own.shape
    shape = jax.ShapeDtypeStruct((2 * window * occupied, 2 * virtual), jnp.bfloat16)
    vmem = pl.BlockSpec(memory_space=pltpu.VMEM)
    return pl.pallas_call(
        spin_kernel,
        out_shape=(shape, shape),
        in_specs=[pl.BlockSpec(memory_space=pltpu.SMEM), vmem, vmem, vmem],
        out_specs=(vmem, vmem),
        scratch_shapes=[pltpu.VMEM((occupied, virtual), jnp.float32)],
        compiler_params=pltpu.CompilerParams(vmem_limit_bytes=40 * MIB),
    )(xl, own, other, swapped)


def product_kernel(xl_ref, high_ref, low_ref, columns_ref, out_ref):
    xl = xl_ref[0]
    blocks, virtual, lanes = columns_ref.shape
    half = lanes // 2
    total = None
    for j in range(2):
        block = jnp.concatenate(
            [columns_ref[z, :, j * half:(j + 1) * half] for z in range(blocks)], axis=1
        )
        high = block.astype(jnp.bfloat16)
        low = (block - high.astype(jnp.float32)).astype(jnp.bfloat16)
        left_high = high_ref[:, j * virtual:(j + 1) * virtual]
        left_low = low_ref[:, j * virtual:(j + 1) * virtual]
        for left, right in ((left_high, low), (left_low, high), (left_high, high)):
            part = jnp.dot(left, right, preferred_element_type=jnp.float32)
            total = part if total is None else total + part
    cores, _, ys, window, local = out_ref.shape[:5]
    for rel in range(2):
        target = xl if rel == 0 else 1 - xl
        for a in range(window):
            for y in range(ys):
                for core in range(cores):
                    start = ((rel * window + a) * ys * cores + y * cores + core) * local
                    out_ref[core, target, y, a] = total[start:start + local]


def product(xl, high, low, columns, ys, window, local):
    steps = 3
    zs, virtual, lanes = columns.shape
    blocks = zs // steps
    width = blocks * lanes // 2
    rows, depth = high.shape
    out = jax.ShapeDtypeStruct((2, 2, ys, window, local, steps * width), jnp.float32)
    return pl.pallas_call(
        product_kernel,
        grid=(steps,),
        out_shape=out,
        in_specs=[
            pl.BlockSpec(memory_space=pltpu.SMEM),
            pl.BlockSpec((rows, depth), lambda n: (0, 0)),
            pl.BlockSpec((rows, depth), lambda n: (0, 0)),
            pl.BlockSpec((blocks, virtual, lanes), lambda n: (n, 0, 0)),
        ],
        out_specs=pl.BlockSpec((2, 2, ys, window, local, width), lambda n: (0, 0, 0, 0, 0, n)),
        compiler_params=pltpu.CompilerParams(vmem_limit_bytes=40 * MIB),
    )(xl, high, low, columns)


def body(amplitudes, integrals, a_irrep, b_irrep, occ_irrep):
    window, occupied, local, virtual = amplitudes.shape
    share, _, width = integrals.shape
    ys = lax.axis_size("y")
    xl = lax.axis_index("xl")
    orb = lax.axis_index("y") * 2 + lax.axis_index("core")
    orbs = 2 * ys

    sent = integrals.reshape(share, orbs, 2, 2, width).transpose(2, 1, 3, 0, 4)
    sent = jnp.broadcast_to(sent[None], (2,) + sent.shape).reshape(4 * orbs, -1)
    got = lax.all_to_all(sent, ("xh", "xl", "y", "core"), 0, 0, tiled=True)
    got = got.reshape(4, orbs, 2, share, width).transpose(1, 3, 2, 0, 4).reshape(virtual, 8 * width)
    columns = lax.all_gather(got, "z", axis=0)

    direct = amplitudes.transpose(2, 0, 1, 3)
    own = lax.dynamic_slice_in_dim(direct, 2 * xl, 2)
    given = lax.dynamic_slice_in_dim(direct, 2 * (1 - xl), 2)
    other = lax.ppermute(given, "xl", [(0, 1), (1, 0)])
    swapped = amplitudes.transpose(1, 0, 2, 3).reshape(2 * orbs, 2, window, local, virtual)
    swapped, _ = lax.optimization_barrier((swapped, got))
    swapped = lax.all_to_all(swapped, ("y", "core", "xl"), 0, 0, tiled=True)

    xl_ref = xl.astype(jnp.int32).reshape(1)
    high, low = spin_rows(xl_ref, own, other, swapped)
    partial = product(xl_ref, high, low, columns, ys, window, local)

    partial = lax.all_to_all(partial, "core", 0, 0, tiled=True)
    partial = (partial[0] + partial[1]).reshape(2 * ys, window, local, -1)
    partial = lax.all_to_all(partial, ("xl", "y"), 0, 0, tiled=True)
    shares = jnp.sum(partial, axis=0)
    zs = columns.shape[0]
    shares = shares.reshape(window, local, zs, 4, width).transpose(0, 1, 3, 2, 4).reshape(window, local, -1)

    local_occ = lax.dynamic_slice_in_dim(occ_irrep, orb * local, local)
    col_sym = jnp.bitwise_xor(b_irrep[:, None], occ_irrep[None, :]).reshape(-1)
    symmetry = jnp.bitwise_xor(
        jnp.bitwise_xor(a_irrep[:, None, None], local_occ[None, :, None]), col_sym[None, None, :]
    )
    return jnp.where(symmetry == 0, shares, jnp.float32(0.0))


def solution(mesh):
    split = Mesh(mesh.devices.reshape(2, 2, 12, 8, 2), ("xh", "xl", "z", "y", "core"))
    pair, orb = ("xh", "xl", "z"), ("y", "core")
    placed = (P(pair, None, orb, None), P(orb, None, pair), P(pair), P(), P())
    return jax.shard_map(
        body, mesh=split, in_specs=placed, out_specs=P(pair, orb, None), check_vma=False
    )
```

```python
import jax
import jax.numpy as jnp
from jax import lax
from jax.experimental import pallas as pl
from jax.experimental.pallas import tpu as pltpu
from jax.sharding import Mesh, PartitionSpec as P

MIB = 1 << 20
VMEM = pl.BlockSpec(memory_space=pltpu.VMEM)


def pack_integrals_kernel(in_ref, out_ref):
    share, _, occupied = in_ref.shape
    half = share // 2
    for xl in range(2):
        for c in range(0, half, 2):
            first = xl * half + c
            pair = jnp.concatenate([in_ref[first], in_ref[first + 1]], axis=1)
            for xh in range(2):
                out_ref[2 * xh + xl, :, c * occupied:(c + 2) * occupied] = pair


def pack_integrals(integrals):
    share, occupied, width = integrals.shape
    return pl.pallas_call(
        pack_integrals_kernel,
        out_shape=jax.ShapeDtypeStruct((4, width, share // 2 * occupied), jnp.float32),
        in_specs=[VMEM],
        out_specs=VMEM,
    )(integrals.transpose(0, 2, 1))


def pack_amplitudes_kernel(in_ref, out_ref, rows, turned, mixed):
    _, occupied, local, virtual = in_ref.shape
    targets, _, depth, lanes = out_ref.shape
    tiles = range(virtual // lanes)
    for d1 in range(occupied):
        for t in tiles:
            rows[t, pl.ds(local * d1, local), :] = in_ref[0, d1, :, t * lanes:(t + 1) * lanes]
    for d2 in range(0, local, 2):
        for t in tiles:
            both = [rows[t, pl.ds(d2 + s, occupied, stride=local), :] for s in range(2)]
            turned[pl.ds(t * lanes, lanes), :] = jnp.concatenate(both, axis=0).T
        even = turned[pl.ds(0, virtual // 2, stride=2), :]
        odd = turned[pl.ds(1, virtual // 2, stride=2), :]
        for s in range(2):
            at = slice(s * occupied, (s + 1) * occupied)
            mixed[pl.ds(d2 + s, virtual // 2, stride=local), :] = jnp.concatenate(
                [even[:, at], odd[:, at]], axis=1
            )
    for target in range(targets):
        out_ref[target, 0] = mixed[pl.ds(depth * target, depth), :]


def pack_amplitudes(amplitudes, targets):
    window, occupied, local, virtual = amplitudes.shape
    depth = virtual // targets // 2 * local
    return pl.pallas_call(
        pack_amplitudes_kernel,
        grid=(window,),
        out_shape=jax.ShapeDtypeStruct((targets, window, depth, 2 * occupied), jnp.float32),
        in_specs=[pl.BlockSpec((1, occupied, local, virtual), lambda a: (a, 0, 0, 0))],
        out_specs=pl.BlockSpec((targets, 1, depth, 2 * occupied), lambda a: (0, a, 0, 0)),
        scratch_shapes=[
            pltpu.VMEM((virtual // (2 * occupied), occupied * local, 2 * occupied), jnp.float32),
            pltpu.VMEM((virtual, 2 * occupied), jnp.float32),
            pltpu.VMEM((virtual // 2 * local, 2 * occupied), jnp.float32),
        ],
        compiler_params=pltpu.CompilerParams(vmem_limit_bytes=16 * MIB),
        cost_estimate=pl.CostEstimate(
            flops=0, bytes_accessed=8 * amplitudes.size, transcendentals=0
        ),
    )(amplitudes)


def spin_kernel(in_ref, high_ref, low_ref, block):
    sources, window, depth, lanes = in_ref.shape
    occupied = lanes // 2
    local = 2 * occupied // sources
    for xl in range(2):
        for a in range(window):
            row = (xl * window + a) * occupied
            for c in range(depth // local):
                for orb in range(sources // 2):
                    block[c % 2, pl.ds(local * orb, local), :] = in_ref[
                        2 * orb + xl, a, c * local:(c + 1) * local
                    ]
                swapped = block[c % 2]
                turned = swapped.T
                direct = jnp.concatenate([turned[:occupied], turned[occupied:]], axis=1)
                spin = 2.0 * direct - swapped
                high = spin.astype(jnp.bfloat16)
                at = (slice(row, row + occupied), slice(c * lanes, (c + 1) * lanes))
                high_ref[at] = high
                low_ref[at] = (spin - high.astype(jnp.float32)).astype(jnp.bfloat16)


def spin_rows(got):
    sources, window, depth, lanes = got.shape
    occupied = lanes // 2
    local = 2 * occupied // sources
    shape = jax.ShapeDtypeStruct((2 * window * occupied, depth // local * lanes), jnp.bfloat16)
    return pl.pallas_call(
        spin_kernel,
        out_shape=(shape, shape),
        in_specs=[VMEM],
        out_specs=(VMEM, VMEM),
        scratch_shapes=[pltpu.VMEM((2, occupied, lanes), jnp.float32)],
        compiler_params=pltpu.CompilerParams(vmem_limit_bytes=16 * MIB),
        cost_estimate=pl.CostEstimate(flops=0, bytes_accessed=8 * got.size, transcendentals=0),
    )(got)


def product_kernel(high_ref, low_ref, columns_ref, out_ref, right_high, right_low):
    zs, _, xls, width, _ = columns_ref.shape
    for xl in range(xls):
        for z in range(zs):
            at = pl.ds((xl * zs + z) * width, width)
            block = columns_ref[z, 0, xl]
            high = block.astype(jnp.bfloat16)
            right_high[at] = high
            right_low[at] = (block - high.astype(jnp.float32)).astype(jnp.bfloat16)

    def dot(left, right):
        return lax.dot_general(
            left[...], right[...], (((1,), (1,)), ((), ())), preferred_element_type=jnp.float32
        )

    total = dot(high_ref, right_low) + dot(low_ref, right_high) + dot(high_ref, right_high)
    cores, _, ys, window, local = out_ref.shape[:5]
    for xl in range(xls):
        for a in range(window):
            for y in range(ys):
                for core in range(cores):
                    start = (((xl * window + a) * ys + y) * cores + core) * local
                    out_ref[core, xl, y, a] = total[start:start + local]


def product(high, low, columns, ys, window, local):
    zs, xhs, xls, width, depth = columns.shape
    rows = high.shape[0]
    block = xls * zs * width
    return pl.pallas_call(
        product_kernel,
        grid=(xhs,),
        out_shape=jax.ShapeDtypeStruct((2, xls, ys, window, local, xhs * block), jnp.float32),
        in_specs=[
            pl.BlockSpec((rows, depth), lambda n: (0, 0)),
            pl.BlockSpec((rows, depth), lambda n: (0, 0)),
            pl.BlockSpec((zs, 1, xls, width, depth), lambda n: (0, n, 0, 0, 0)),
        ],
        out_specs=pl.BlockSpec((2, xls, ys, window, local, block), lambda n: (0, 0, 0, 0, 0, n)),
        scratch_shapes=[pltpu.VMEM((block, depth), jnp.bfloat16)] * 2,
        compiler_params=pltpu.CompilerParams(vmem_limit_bytes=60 * MIB),
        cost_estimate=pl.CostEstimate(
            flops=6 * rows * depth * xhs * block, bytes_accessed=8 << 20, transcendentals=0
        ),
    )(high, low, columns)


def body(amplitudes, integrals, a_irrep, b_irrep, occ_irrep):
    window, occupied, local, virtual = amplitudes.shape
    ys = lax.axis_size("y")
    orb = lax.axis_index("y") * 2 + lax.axis_index("core")

    sent = pack_integrals(integrals)
    got = lax.all_to_all(sent, ("xh", "xl"), 0, 0, tiled=True)
    columns = lax.all_gather(got.reshape((2, 2) + got.shape[1:]), "z", axis=0)

    packed = pack_amplitudes(amplitudes, 4 * ys)
    packed, _ = lax.optimization_barrier((packed, got))
    packed = lax.all_to_all(packed, ("y", "core", "xl"), 0, 0, tiled=True)

    high, low = spin_rows(packed)
    partial = product(high, low, columns, ys, window, local)

    partial = lax.all_to_all(partial, "core", 0, 0, tiled=True)
    partial = (partial[0] + partial[1]).reshape(2 * ys, window, local, -1)
    partial = lax.all_to_all(partial, ("xl", "y"), 0, 0, tiled=True)
    shares = jnp.sum(partial, axis=0)

    local_occ = lax.dynamic_slice_in_dim(occ_irrep, orb * local, local)
    col_sym = jnp.bitwise_xor(b_irrep[:, None], occ_irrep[None, :]).reshape(-1)
    symmetry = jnp.bitwise_xor(
        jnp.bitwise_xor(a_irrep[:, None, None], local_occ[None, :, None]), col_sym[None, None, :]
    )
    return jnp.where(symmetry == 0, shares, jnp.float32(0.0))


def solution(mesh):
    split = Mesh(mesh.devices.reshape(2, 2, 12, 8, 2), ("xh", "xl", "z", "y", "core"))
    pair, orb = ("xh", "xl", "z"), ("y", "core")
    placed = (P(pair, None, orb, None), P(orb, None, pair), P(pair), P(), P())
    return jax.shard_map(
        body, mesh=split, in_specs=placed, out_specs=P(pair, orb, None), check_vma=False
    )
```

```python
import jax
import jax.numpy as jnp
from jax import lax
from jax.experimental import pallas as pl
from jax.experimental.pallas import tpu as pltpu
from jax.sharding import Mesh, PartitionSpec as P

MIB = 1 << 20
VMEM = pl.BlockSpec(memory_space=pltpu.VMEM)


def pack_integrals_kernel(in_ref, out_ref):
    share, _, occupied = in_ref.shape
    half = share // 2
    for xl in range(2):
        for c in range(0, half, 2):
            first = xl * half + c
            pair = jnp.concatenate([in_ref[first], in_ref[first + 1]], axis=1)
            for xh in range(2):
                out_ref[2 * xh + xl, :, c * occupied:(c + 2) * occupied] = pair


def pack_integrals(integrals):
    share, occupied, width = integrals.shape
    return pl.pallas_call(
        pack_integrals_kernel,
        out_shape=jax.ShapeDtypeStruct((4, width, share // 2 * occupied), jnp.float32),
        in_specs=[VMEM],
        out_specs=VMEM,
    )(integrals.transpose(0, 2, 1))


def pack_amplitudes_kernel(in_ref, out_ref, rows, turned, mixed):
    _, occupied, local, virtual = in_ref.shape
    targets, _, depth, lanes = out_ref.shape
    tiles = range(virtual // lanes)
    for d1 in range(occupied):
        for t in tiles:
            rows[t, pl.ds(local * d1, local), :] = in_ref[0, d1, :, t * lanes:(t + 1) * lanes]
    for d2 in range(0, local, 2):
        for t in tiles:
            both = [rows[t, pl.ds(d2 + s, occupied, stride=local), :] for s in range(2)]
            turned[pl.ds(t * lanes, lanes), :] = jnp.concatenate(both, axis=0).T
        even = turned[pl.ds(0, virtual // 2, stride=2), :]
        odd = turned[pl.ds(1, virtual // 2, stride=2), :]
        for s in range(2):
            at = slice(s * occupied, (s + 1) * occupied)
            mixed[pl.ds(d2 + s, virtual // 2, stride=local), :] = jnp.concatenate(
                [even[:, at], odd[:, at]], axis=1
            )
    for target in range(targets):
        out_ref[target, 0] = mixed[pl.ds(depth * target, depth), :]


def pack_amplitudes(amplitudes, targets):
    window, occupied, local, virtual = amplitudes.shape
    depth = virtual // targets // 2 * local
    return pl.pallas_call(
        pack_amplitudes_kernel,
        grid=(window,),
        out_shape=jax.ShapeDtypeStruct((targets, window, depth, 2 * occupied), jnp.float32),
        in_specs=[pl.BlockSpec((1, occupied, local, virtual), lambda a: (a, 0, 0, 0))],
        out_specs=pl.BlockSpec((targets, 1, depth, 2 * occupied), lambda a: (0, a, 0, 0)),
        scratch_shapes=[
            pltpu.VMEM((virtual // (2 * occupied), occupied * local, 2 * occupied), jnp.float32),
            pltpu.VMEM((virtual, 2 * occupied), jnp.float32),
            pltpu.VMEM((virtual // 2 * local, 2 * occupied), jnp.float32),
        ],
        compiler_params=pltpu.CompilerParams(vmem_limit_bytes=16 * MIB),
        cost_estimate=pl.CostEstimate(
            flops=0, bytes_accessed=8 * amplitudes.size, transcendentals=0
        ),
    )(amplitudes)


def spin_kernel(in_ref, high_ref, low_ref, block, mixed):
    sources, window, depth, lanes = in_ref.shape
    occupied = lanes // 2
    orbs = sources // 2
    local = occupied // orbs
    for xl in range(2):
        for a in range(window):
            row = (xl * window + a) * occupied // 2
            for c in range(depth // local):
                slot = c % 2
                for orb in range(orbs):
                    block[slot, pl.ds(local * orb, local), :] = in_ref[
                        2 * orb + xl, a, c * local:(c + 1) * local
                    ]
                swapped = block[slot]
                turned = swapped.T
                direct = jnp.concatenate([turned[:occupied], turned[occupied:]], axis=1)
                spin = 2.0 * direct - swapped
                for orb in range(orbs):
                    to = (orb % 2) * occupied // 2 + orb // 2 * local
                    mixed[slot, pl.ds(to, local), :] = spin[local * orb:local * (orb + 1)]
                for core in range(2):
                    rows = mixed[slot, pl.ds(core * occupied // 2, occupied // 2), :]
                    high = rows.astype(jnp.bfloat16)
                    at = (core, slice(row, row + occupied // 2), slice(c * lanes, (c + 1) * lanes))
                    high_ref[at] = high
                    low_ref[at] = (rows - high.astype(jnp.float32)).astype(jnp.bfloat16)


def spin_rows(got):
    sources, window, depth, lanes = got.shape
    occupied = lanes // 2
    local = 2 * occupied // sources
    shape = jax.ShapeDtypeStruct((2, window * occupied, depth // local * lanes), jnp.bfloat16)
    return pl.pallas_call(
        spin_kernel,
        out_shape=(shape, shape),
        in_specs=[VMEM],
        out_specs=(VMEM, VMEM),
        scratch_shapes=[pltpu.VMEM((2, occupied, lanes), jnp.float32)] * 2,
        compiler_params=pltpu.CompilerParams(vmem_limit_bytes=8 * MIB),
        cost_estimate=pl.CostEstimate(flops=0, bytes_accessed=8 * got.size, transcendentals=0),
    )(got)


def product_kernel(
    core_ref, high_ref, low_ref, columns_ref, out_ref, left, right, right_high, right_low, sems
):
    zs, xs, width, depth = columns_ref.shape
    core = core_ref[0]
    copies = [
        pltpu.make_async_copy(columns_ref.at[:, x], right.at[x], sems.at[x]) for x in range(xs)
    ]
    halves = [
        pltpu.make_async_copy(ref.at[core], left.at[i], sems.at[xs + i])
        for i, ref in enumerate((high_ref, low_ref))
    ]
    for copy in copies[:1] + halves + copies[1:]:
        copy.start()
    block = xs // 2 * zs * width
    xls, ys, window, local = out_ref.shape[:4]

    def dot(left, right):
        return lax.dot_general(
            left, right, (((1,), (1,)), ((), ())), preferred_element_type=jnp.float32
        )

    for side in range(2):
        for x in range(side * xs // 2, (side + 1) * xs // 2):
            copies[x].wait()
            for z in range(zs):
                at = pl.ds((x * zs + z) * width, width)
                rows = right[x, z]
                high = rows.astype(jnp.bfloat16)
                right_high[at] = high
                right_low[at] = (rows - high.astype(jnp.float32)).astype(jnp.bfloat16)
        if side == 0:
            for copy in halves:
                copy.wait()
        left_high, left_low = left[0], left[1]
        at = pl.ds(side * block, block)
        high, low = right_high[at], right_low[at]
        total = dot(left_high, low) + dot(left_low, high) + dot(left_high, high)
        for xl in range(xls):
            for a in range(window):
                for y in range(ys):
                    start = ((xl * window + a) * ys + y) * local
                    out_ref[xl, y, a, :, side * block:(side + 1) * block] = total[start:start + local]


def product(core, high, low, columns, ys, window, local):
    zs, xs, width, depth = columns.shape
    rows = high.shape[1]
    return pl.pallas_call(
        product_kernel,
        out_shape=jax.ShapeDtypeStruct((2, ys, window, local, xs * zs * width), jnp.float32),
        in_specs=[pl.BlockSpec(memory_space=pltpu.SMEM)] + [pl.BlockSpec(memory_space=pl.ANY)] * 3,
        out_specs=VMEM,
        scratch_shapes=[
            pltpu.VMEM((2, rows, depth), jnp.bfloat16),
            pltpu.VMEM((xs, zs, width, depth), jnp.float32),
            pltpu.VMEM((xs * zs * width, depth), jnp.bfloat16),
            pltpu.VMEM((xs * zs * width, depth), jnp.bfloat16),
            pltpu.SemaphoreType.DMA((xs + 2,)),
        ],
        compiler_params=pltpu.CompilerParams(vmem_limit_bytes=52 * MIB),
        cost_estimate=pl.CostEstimate(
            flops=6 * rows * depth * xs * zs * width, bytes_accessed=8 << 20, transcendentals=0
        ),
    )(core, high, low, columns)


def body(amplitudes, integrals, a_irrep, b_irrep, occ_irrep):
    window, occupied, local, virtual = amplitudes.shape
    ys = lax.axis_size("y")
    orb = lax.axis_index("y") * 2 + lax.axis_index("core")

    sent = pack_integrals(integrals)
    got = lax.all_to_all(sent, ("xh", "xl"), 0, 0, tiled=True)
    packed = pack_amplitudes(amplitudes, 4 * ys)
    packed, got = lax.optimization_barrier((packed, got))
    columns = lax.all_gather(got, "z", axis=0)

    packed = lax.all_to_all(packed, ("y", "core", "xl"), 0, 0, tiled=True)
    high, low = spin_rows(packed)

    core = lax.axis_index("core").astype(jnp.int32).reshape(1)
    given = product(1 - core, high, low, columns, ys, window, local)
    given = lax.ppermute(given, "core", [(0, 1), (1, 0)])
    partial = product(core, high, low, columns, ys, window, local) + given

    partial = partial.reshape(2 * ys, window, local, -1)
    partial = lax.all_to_all(partial, ("xl", "y"), 0, 0, tiled=True)
    shares = jnp.sum(partial, axis=0)

    local_occ = lax.dynamic_slice_in_dim(occ_irrep, orb * local, local)
    col_sym = jnp.bitwise_xor(b_irrep[:, None], occ_irrep[None, :]).reshape(-1)
    symmetry = jnp.bitwise_xor(
        jnp.bitwise_xor(a_irrep[:, None, None], local_occ[None, :, None]), col_sym[None, None, :]
    )
    return jnp.where(symmetry == 0, shares, jnp.float32(0.0))


def solution(mesh):
    split = Mesh(mesh.devices.reshape(2, 2, 12, 8, 2), ("xh", "xl", "z", "y", "core"))
    pair, orb = ("xh", "xl", "z"), ("y", "core")
    placed = (P(pair, None, orb, None), P(orb, None, pair), P(pair), P(), P())
    return jax.shard_map(
        body, mesh=split, in_specs=placed, out_specs=P(pair, orb, None), check_vma=False
    )
```

```python
import jax
import jax.numpy as jnp
from jax import lax
from jax.experimental import pallas as pl
from jax.experimental.pallas import tpu as pltpu
from jax.sharding import Mesh, PartitionSpec as P

MIB = 1 << 20
VMEM = pl.BlockSpec(memory_space=pltpu.VMEM)


def pack_integrals_kernel(in_ref, out_ref):
    share, _, occupied = in_ref.shape
    half = share // 2
    for xl in range(2):
        for c in range(0, half, 2):
            first = xl * half + c
            pair = jnp.concatenate([in_ref[first], in_ref[first + 1]], axis=1)
            for xh in range(2):
                out_ref[2 * xh + xl, :, c * occupied:(c + 2) * occupied] = pair


def pack_integrals(integrals):
    share, occupied, width = integrals.shape
    return pl.pallas_call(
        pack_integrals_kernel,
        out_shape=jax.ShapeDtypeStruct((4, width, share // 2 * occupied), jnp.float32),
        in_specs=[VMEM],
        out_specs=VMEM,
    )(integrals.transpose(0, 2, 1))


def pack_amplitudes_kernel(in_ref, out_ref, rows, turned, mixed):
    _, occupied, local, virtual = in_ref.shape
    targets, _, depth, lanes = out_ref.shape
    tiles = range(virtual // lanes)
    for d1 in range(occupied):
        for t in tiles:
            rows[t, pl.ds(local * d1, local), :] = in_ref[0, d1, :, t * lanes:(t + 1) * lanes]
    for d2 in range(0, local, 2):
        for t in tiles:
            both = [rows[t, pl.ds(d2 + s, occupied, stride=local), :] for s in range(2)]
            turned[pl.ds(t * lanes, lanes), :] = jnp.concatenate(both, axis=0).T
        even = turned[pl.ds(0, virtual // 2, stride=2), :]
        odd = turned[pl.ds(1, virtual // 2, stride=2), :]
        for s in range(2):
            at = slice(s * occupied, (s + 1) * occupied)
            mixed[pl.ds(d2 + s, virtual // 2, stride=local), :] = jnp.concatenate(
                [even[:, at], odd[:, at]], axis=1
            )
    for target in range(targets):
        out_ref[target, 0] = mixed[pl.ds(depth * target, depth), :]


def pack_amplitudes(amplitudes, targets):
    window, occupied, local, virtual = amplitudes.shape
    depth = virtual // targets // 2 * local
    return pl.pallas_call(
        pack_amplitudes_kernel,
        grid=(window,),
        out_shape=jax.ShapeDtypeStruct((targets, window, depth, 2 * occupied), jnp.float32),
        in_specs=[pl.BlockSpec((1, occupied, local, virtual), lambda a: (a, 0, 0, 0))],
        out_specs=pl.BlockSpec((targets, 1, depth, 2 * occupied), lambda a: (0, a, 0, 0)),
        scratch_shapes=[
            pltpu.VMEM((virtual // (2 * occupied), occupied * local, 2 * occupied), jnp.float32),
            pltpu.VMEM((virtual, 2 * occupied), jnp.float32),
            pltpu.VMEM((virtual // 2 * local, 2 * occupied), jnp.float32),
        ],
        compiler_params=pltpu.CompilerParams(vmem_limit_bytes=16 * MIB),
        cost_estimate=pl.CostEstimate(
            flops=0, bytes_accessed=8 * amplitudes.size, transcendentals=0
        ),
    )(amplitudes)


def spin_kernel(in_ref, high_ref, low_ref, block, mixed):
    sources, window, depth, lanes = in_ref.shape
    occupied = lanes // 2
    orbs = sources // 2
    local = occupied // orbs
    for xl in range(2):
        for a in range(window):
            row = (xl * window + a) * occupied // 2
            for c in range(depth // local):
                slot = c % 2
                for orb in range(orbs):
                    block[slot, pl.ds(local * orb, local), :] = in_ref[
                        2 * orb + xl, a, c * local:(c + 1) * local
                    ]
                swapped = block[slot]
                turned = swapped.T
                direct = jnp.concatenate([turned[:occupied], turned[occupied:]], axis=1)
                spin = 2.0 * direct - swapped
                for orb in range(orbs):
                    to = (orb % 2) * occupied // 2 + orb // 2 * local
                    mixed[slot, pl.ds(to, local), :] = spin[local * orb:local * (orb + 1)]
                for core in range(2):
                    rows = mixed[slot, pl.ds(core * occupied // 2, occupied // 2), :]
                    high = rows.astype(jnp.bfloat16)
                    at = (core, slice(row, row + occupied // 2), slice(c * lanes, (c + 1) * lanes))
                    high_ref[at] = high
                    low_ref[at] = (rows - high.astype(jnp.float32)).astype(jnp.bfloat16)


def spin_rows(got):
    sources, window, depth, lanes = got.shape
    occupied = lanes // 2
    local = 2 * occupied // sources
    shape = jax.ShapeDtypeStruct((2, window * occupied, depth // local * lanes), jnp.bfloat16)
    return pl.pallas_call(
        spin_kernel,
        out_shape=(shape, shape),
        in_specs=[VMEM],
        out_specs=(VMEM, VMEM),
        scratch_shapes=[pltpu.VMEM((2, occupied, lanes), jnp.float32)] * 2,
        compiler_params=pltpu.CompilerParams(vmem_limit_bytes=8 * MIB),
        cost_estimate=pl.CostEstimate(flops=0, bytes_accessed=8 * got.size, transcendentals=0),
    )(got)


def product_kernel(place_ref, high_ref, low_ref, *refs):
    *columns_refs, own_ref, other_ref, left, right, right_high, right_low, sems = refs
    zs = len(columns_refs)
    xs, width = columns_refs[0].shape[:2]
    z, core = place_ref[0], place_ref[1]
    rows = high_ref.shape[1]
    copies = [
        pltpu.make_async_copy(ref, right.at[r], sems.at[r]) for r, ref in enumerate(columns_refs)
    ]
    halves = [
        pltpu.make_async_copy(
            ref.at[side], left.at[i, pl.ds(part * rows, rows)], sems.at[zs + 2 * i + part]
        )
        for i, ref in enumerate((high_ref, low_ref))
        for part, side in enumerate((core, 1 - core))
    ]
    for copy in copies + halves:
        copy.start()
    for r in range(zs):
        copies[r].wait()
        at_z = lax.rem(z + r, zs)
        for x in range(xs):
            at = pl.ds(pl.multiple_of((x * zs + at_z) * width, width), width)
            block = right[r, x]
            high = block.astype(jnp.bfloat16)
            right_high[at] = high
            right_low[at] = (block - high.astype(jnp.float32)).astype(jnp.bfloat16)

    def dot(left, right):
        return lax.dot_general(
            left, right[...], (((1,), (1,)), ((), ())), preferred_element_type=jnp.float32
        )

    for copy in halves:
        copy.wait()
    total = dot(left[0], right_low) + dot(left[1], right_high) + dot(left[0], right_high)
    ys, xls, window, local = own_ref.shape[:4]
    for i, ref in enumerate((own_ref, other_ref)):
        for xl in range(xls):
            for a in range(window):
                for y in range(ys):
                    start = i * rows + ((xl * window + a) * ys + y) * local
                    ref[y, xl, a] = total[start:start + local]


def product(place, high, low, columns, ys, window, local):
    xs, width, depth = columns[0].shape
    rows = high.shape[1]
    block = xs * len(columns) * width
    shape = jax.ShapeDtypeStruct((ys, 2, window, local, block), jnp.float32)
    return pl.pallas_call(
        product_kernel,
        out_shape=(shape, shape),
        in_specs=[pl.BlockSpec(memory_space=pltpu.SMEM)]
        + [pl.BlockSpec(memory_space=pl.ANY)] * (2 + len(columns)),
        out_specs=(VMEM, VMEM),
        scratch_shapes=[
            pltpu.VMEM((2, 2 * rows, depth), jnp.bfloat16),
            pltpu.VMEM((len(columns), xs, width, depth), jnp.float32),
            pltpu.VMEM((block, depth), jnp.bfloat16),
            pltpu.VMEM((block, depth), jnp.bfloat16),
            pltpu.SemaphoreType.DMA((len(columns) + 4,)),
        ],
        compiler_params=pltpu.CompilerParams(vmem_limit_bytes=50 * MIB),
        cost_estimate=pl.CostEstimate(
            flops=12 * rows * depth * block, bytes_accessed=8 << 20, transcendentals=0
        ),
    )(place, high, low, *columns)


def gather(block, axis, hops, sign):
    size = lax.axis_size(axis)
    pairs = [(i, (i - sign) % size) for i in range(size)]
    blocks = [block]
    for _ in range(hops):
        blocks.append(lax.ppermute(blocks[-1], axis, pairs))
    return blocks[1:]


def body(amplitudes, integrals, a_irrep, b_irrep, occ_irrep):
    window, occupied, local, virtual = amplitudes.shape
    ys = lax.axis_size("y")
    orb = lax.axis_index("y") * 2 + lax.axis_index("core")

    local_occ = lax.dynamic_slice_in_dim(occ_irrep, orb * local, local)
    col_sym = jnp.bitwise_xor(b_irrep[:, None], occ_irrep[None, :]).reshape(-1)
    symmetry = jnp.bitwise_xor(
        jnp.bitwise_xor(a_irrep[:, None, None], local_occ[None, :, None]), col_sym[None, None, :]
    )

    sent = pack_integrals(integrals)
    got = lax.all_to_all(sent, ("xh", "xl"), 0, 0, tiled=True)
    half = lax.axis_size("z") // 2
    ahead = gather(got, "z", half - 1, 1)
    behind = gather(got, "z", half - 1, -1)

    packed = pack_amplitudes(amplitudes, 4 * ys)
    packed, _ = lax.optimization_barrier((packed, got))
    packed = lax.all_to_all(packed, ("y", "core", "xl"), 0, 0, tiled=True)
    packed, symmetry = lax.optimization_barrier((packed, symmetry))
    high, low = spin_rows(packed)
    last, high, low = lax.optimization_barrier((ahead[-1], high, low))
    ahead += gather(last, "z", 1, 1)

    place = jnp.stack([lax.axis_index("z"), lax.axis_index("core")]).astype(jnp.int32)
    columns = [got] + ahead + behind[::-1]
    partial, given = product(place, high, low, columns, ys, window, local)
    partial = partial + lax.ppermute(given, "core", [(0, 1), (1, 0)])

    partial = partial.reshape(2 * ys, window, local, -1)
    partial = lax.all_to_all(partial, ("y", "xl"), 0, 0, tiled=True)
    shares = jnp.sum(partial, axis=0)
    return jnp.where(symmetry == 0, shares, jnp.float32(0.0))


def solution(mesh):
    split = Mesh(mesh.devices.reshape(2, 2, 12, 8, 2), ("xh", "xl", "z", "y", "core"))
    pair, orb = ("xh", "xl", "z"), ("y", "core")
    placed = (P(pair, None, orb, None), P(orb, None, pair), P(pair), P(), P())
    return jax.shard_map(
        body, mesh=split, in_specs=placed, out_specs=P(pair, orb, None), check_vma=False
    )
```

```python
import jax
import jax.numpy as jnp
from jax import lax
from jax.experimental import pallas as pl
from jax.experimental.pallas import tpu as pltpu
from jax.sharding import Mesh, PartitionSpec as P

MIB = 1 << 20
VMEM = pl.BlockSpec(memory_space=pltpu.VMEM)


def pack_integrals_kernel(in_ref, out_ref):
    share, _, occupied = in_ref.shape
    half = share // 2
    for xl in range(2):
        for c in range(0, half, 2):
            first = xl * half + c
            pair = jnp.concatenate([in_ref[first], in_ref[first + 1]], axis=1)
            for xh in range(2):
                out_ref[2 * xh + xl, :, c * occupied:(c + 2) * occupied] = pair


def pack_integrals(integrals):
    share, occupied, width = integrals.shape
    return pl.pallas_call(
        pack_integrals_kernel,
        out_shape=jax.ShapeDtypeStruct((4, width, share // 2 * occupied), jnp.float32),
        in_specs=[VMEM],
        out_specs=VMEM,
    )(integrals.transpose(0, 2, 1))


def pack_amplitudes_kernel(in_ref, out_ref, rows, turned, mixed):
    _, occupied, local, virtual = in_ref.shape
    targets, _, depth, lanes = out_ref.shape
    tiles = range(virtual // lanes)
    for d1 in range(occupied):
        for t in tiles:
            rows[t, pl.ds(local * d1, local), :] = in_ref[0, d1, :, t * lanes:(t + 1) * lanes]
    for d2 in range(0, local, 2):
        for t in tiles:
            both = [rows[t, pl.ds(d2 + s, occupied, stride=local), :] for s in range(2)]
            turned[pl.ds(t * lanes, lanes), :] = jnp.concatenate(both, axis=0).T
        even = turned[pl.ds(0, virtual // 2, stride=2), :]
        odd = turned[pl.ds(1, virtual // 2, stride=2), :]
        for s in range(2):
            at = slice(s * occupied, (s + 1) * occupied)
            mixed[pl.ds(d2 + s, virtual // 2, stride=local), :] = jnp.concatenate(
                [even[:, at], odd[:, at]], axis=1
            )
    for target in range(targets):
        out_ref[target, 0] = mixed[pl.ds(depth * target, depth), :]


def pack_amplitudes(amplitudes, targets):
    window, occupied, local, virtual = amplitudes.shape
    depth = virtual // targets // 2 * local
    return pl.pallas_call(
        pack_amplitudes_kernel,
        grid=(window,),
        out_shape=jax.ShapeDtypeStruct((targets, window, depth, 2 * occupied), jnp.float32),
        in_specs=[pl.BlockSpec((1, occupied, local, virtual), lambda a: (a, 0, 0, 0))],
        out_specs=pl.BlockSpec((targets, 1, depth, 2 * occupied), lambda a: (0, a, 0, 0)),
        scratch_shapes=[
            pltpu.VMEM((virtual // (2 * occupied), occupied * local, 2 * occupied), jnp.float32),
            pltpu.VMEM((virtual, 2 * occupied), jnp.float32),
            pltpu.VMEM((virtual // 2 * local, 2 * occupied), jnp.float32),
        ],
        compiler_params=pltpu.CompilerParams(vmem_limit_bytes=16 * MIB),
        cost_estimate=pl.CostEstimate(
            flops=0, bytes_accessed=8 * amplitudes.size, transcendentals=0
        ),
    )(amplitudes)


def spin_kernel(in_ref, high_ref, low_ref, block, mixed):
    sources, window, depth, lanes = in_ref.shape
    occupied = lanes // 2
    orbs = sources // 2
    local = occupied // orbs
    for xl in range(2):
        for a in range(window):
            row = (xl * window + a) * occupied // 2
            for c in range(depth // local):
                slot = c % 2
                for orb in range(orbs):
                    block[slot, pl.ds(local * orb, local), :] = in_ref[
                        2 * orb + xl, a, c * local:(c + 1) * local
                    ]
                swapped = block[slot]
                turned = swapped.T
                direct = jnp.concatenate([turned[:occupied], turned[occupied:]], axis=1)
                spin = 2.0 * direct - swapped
                for orb in range(orbs):
                    to = (orb % 2) * occupied // 2 + orb // 2 * local
                    mixed[slot, pl.ds(to, local), :] = spin[local * orb:local * (orb + 1)]
                for core in range(2):
                    rows = mixed[slot, pl.ds(core * occupied // 2, occupied // 2), :]
                    high = rows.astype(jnp.bfloat16)
                    at = (core, slice(row, row + occupied // 2), slice(c * lanes, (c + 1) * lanes))
                    high_ref[at] = high
                    low_ref[at] = (rows - high.astype(jnp.float32)).astype(jnp.bfloat16)


def spin_rows(got):
    sources, window, depth, lanes = got.shape
    occupied = lanes // 2
    local = 2 * occupied // sources
    shape = jax.ShapeDtypeStruct((2, window * occupied, depth // local * lanes), jnp.bfloat16)
    return pl.pallas_call(
        spin_kernel,
        out_shape=(shape, shape),
        in_specs=[VMEM],
        out_specs=(VMEM, VMEM),
        scratch_shapes=[pltpu.VMEM((2, occupied, lanes), jnp.float32)] * 2,
        compiler_params=pltpu.CompilerParams(vmem_limit_bytes=8 * MIB),
        cost_estimate=pl.CostEstimate(flops=0, bytes_accessed=8 * got.size, transcendentals=0),
    )(got)


def product_kernel(core_ref, high_ref, low_ref, *refs):
    *columns_refs, own_ref, other_ref, left, right, right_high, right_low, sems = refs
    count = len(columns_refs)
    xs, width, depth = columns_refs[0].shape
    core = core_ref[0]
    rows = high_ref.shape[1]
    copies = [
        pltpu.make_async_copy(ref, right.at[r], sems.at[r]) for r, ref in enumerate(columns_refs)
    ]
    halves = [
        pltpu.make_async_copy(
            ref.at[side], left.at[i, pl.ds(part * rows, rows)], sems.at[count + 2 * i + part]
        )
        for i, ref in enumerate((high_ref, low_ref))
        for part, side in enumerate((core, 1 - core))
    ]
    for copy in copies[:2] + halves + copies[2:]:
        copy.start()

    def dot(left, right):
        return lax.dot_general(
            left, right, (((1,), (1,)), ((), ())), preferred_element_type=jnp.float32
        )

    ys, xls, window, local = own_ref.shape[:4]
    group = 4
    for first in range(0, count, group):
        for r in range(first, first + group):
            copies[r].wait()
            block = right[r].reshape(xs * width, depth)
            high = block.astype(jnp.bfloat16)
            at = pl.ds(r * xs * width, xs * width)
            right_high[at] = high
            right_low[at] = (block - high.astype(jnp.float32)).astype(jnp.bfloat16)
        if first == 0:
            for copy in halves:
                copy.wait()
        at = pl.ds(first * xs * width, group * xs * width)
        high, low = right_high[at], right_low[at]
        total = dot(left[0], low) + dot(left[1], high) + dot(left[0], high)
        for i, ref in enumerate((own_ref, other_ref)):
            for xl in range(xls):
                for a in range(window):
                    for y in range(ys):
                        start = i * rows + ((xl * window + a) * ys + y) * local
                        ref[y, xl, a, :, first * xs * width:(first + group) * xs * width] = total[
                            start:start + local
                        ]


def product(core, high, low, columns, ys, window, local):
    xs, width, depth = columns[0].shape
    rows = high.shape[1]
    block = xs * len(columns) * width
    shape = jax.ShapeDtypeStruct((ys, 2, window, local, block), jnp.float32)
    return pl.pallas_call(
        product_kernel,
        out_shape=(shape, shape),
        in_specs=[pl.BlockSpec(memory_space=pltpu.SMEM)]
        + [pl.BlockSpec(memory_space=pl.ANY)] * (2 + len(columns)),
        out_specs=(VMEM, VMEM),
        scratch_shapes=[
            pltpu.VMEM((2, 2 * rows, depth), jnp.bfloat16),
            pltpu.VMEM((len(columns), xs, width, depth), jnp.float32),
            pltpu.VMEM((block, depth), jnp.bfloat16),
            pltpu.VMEM((block, depth), jnp.bfloat16),
            pltpu.SemaphoreType.DMA((len(columns) + 4,)),
        ],
        compiler_params=pltpu.CompilerParams(vmem_limit_bytes=53 * MIB),
        cost_estimate=pl.CostEstimate(
            flops=12 * rows * depth * block, bytes_accessed=8 << 20, transcendentals=0
        ),
    )(core, high, low, *columns)


def finish_kernel(z_ref, parts_ref, symmetry_ref, out_ref, rows):
    sources, window, local, columns = parts_ref.shape
    zs = 12
    width = columns // zs
    for a in range(window):
        total = parts_ref[0, a]
        for source in range(1, sources):
            total = total + parts_ref[source, a]
        rows[pl.ds(a * local, local), :] = total
    turned = pltpu.roll(rows[...], lax.rem(z_ref[0] + zs - 4, zs) * width, 1)
    ordered = jnp.concatenate(
        [
            turned[:, z * width + x * 16:z * width + (x + 1) * 16]
            for x in range(width // 16)
            for z in range(zs)
        ],
        axis=1,
    )
    for a in range(window):
        out_ref[a] = jnp.where(
            symmetry_ref[a] == 0, ordered[a * local:(a + 1) * local], jnp.float32(0.0)
        )


def finish(z, parts, symmetry):
    _, window, local, columns = parts.shape
    return pl.pallas_call(
        finish_kernel,
        out_shape=jax.ShapeDtypeStruct((window, local, columns), jnp.float32),
        in_specs=[pl.BlockSpec(memory_space=pltpu.SMEM), VMEM, VMEM],
        out_specs=VMEM,
        scratch_shapes=[pltpu.VMEM((16, columns), jnp.float32)],
        compiler_params=pltpu.CompilerParams(vmem_limit_bytes=8 * MIB),
    )(z, parts, symmetry)


def gather(block, axis, hops, sign):
    size = lax.axis_size(axis)
    pairs = [(i, (i - sign) % size) for i in range(size)]
    blocks = [block]
    for _ in range(hops):
        blocks.append(lax.ppermute(blocks[-1], axis, pairs))
    return blocks[1:]


def body(amplitudes, integrals, a_irrep, b_irrep, occ_irrep):
    window, occupied, local, virtual = amplitudes.shape
    ys = lax.axis_size("y")
    orb = lax.axis_index("y") * 2 + lax.axis_index("core")

    local_occ = lax.dynamic_slice_in_dim(occ_irrep, orb * local, local)
    col_sym = jnp.bitwise_xor(b_irrep[:, None], occ_irrep[None, :]).reshape(-1)
    symmetry = jnp.bitwise_xor(
        jnp.bitwise_xor(a_irrep[:, None, None], local_occ[None, :, None]), col_sym[None, None, :]
    )

    sent = pack_integrals(integrals)
    got = lax.all_to_all(sent, ("xh", "xl"), 0, 0, tiled=True)
    half = lax.axis_size("z") // 2
    ahead = gather(got, "z", half - 1, 1)
    behind = gather(got, "z", half - 1, -1)

    packed = pack_amplitudes(amplitudes, 4 * ys)
    packed, _ = lax.optimization_barrier((packed, got))
    packed = lax.all_to_all(packed, ("y", "core", "xl"), 0, 0, tiled=True)
    packed, symmetry = lax.optimization_barrier((packed, symmetry))
    high, low = spin_rows(packed)
    last, high, low = lax.optimization_barrier((ahead[-1], high, low))
    ahead += gather(last, "z", 1, 1)

    core = lax.axis_index("core").astype(jnp.int32).reshape(1)
    swap = [(0, 1), (1, 0)]
    early = behind[3::-1] + [got] + ahead[:3]
    late = ahead[3:] + behind[4:]
    own, given = product(core, high, low, early, ys, window, local)
    taken = lax.ppermute(given, "core", swap)
    own_late, given = product(core, high, low, late, ys, window, local)
    partial = jnp.concatenate([own + taken, own_late + lax.ppermute(given, "core", swap)], axis=-1)

    partial = partial.reshape(2 * ys, window, local, -1)
    partial = lax.all_to_all(partial, ("y", "xl"), 0, 0, tiled=True)
    z = lax.axis_index("z").astype(jnp.int32).reshape(1)
    return finish(z, partial, symmetry)


def solution(mesh):
    split = Mesh(mesh.devices.reshape(2, 2, 12, 8, 2), ("xh", "xl", "z", "y", "core"))
    pair, orb = ("xh", "xl", "z"), ("y", "core")
    placed = (P(pair, None, orb, None), P(orb, None, pair), P(pair), P(), P())
    return jax.shard_map(
        body, mesh=split, in_specs=placed, out_specs=P(pair, orb, None), check_vma=False
    )
```

```python
import functools

import jax
import jax.numpy as jnp
from jax import lax
from jax.experimental import pallas as pl
from jax.experimental.pallas import tpu as pltpu
from jax.sharding import Mesh, PartitionSpec as P

MIB = 1 << 20
VMEM = pl.BlockSpec(memory_space=pltpu.VMEM)


def pack_integrals_kernel(in_ref, out_ref):
    share, _, occupied = in_ref.shape
    half = share // 2
    for xl in range(2):
        for c in range(0, half, 2):
            first = xl * half + c
            pair = jnp.concatenate([in_ref[first], in_ref[first + 1]], axis=1)
            for xh in range(2):
                out_ref[2 * xh + xl, :, c * occupied:(c + 2) * occupied] = pair


def pack_integrals(integrals):
    share, occupied, width = integrals.shape
    return pl.pallas_call(
        pack_integrals_kernel,
        out_shape=jax.ShapeDtypeStruct((4, width, share // 2 * occupied), jnp.float32),
        in_specs=[VMEM],
        out_specs=VMEM,
    )(integrals.transpose(0, 2, 1))


def pack_amplitudes_kernel(in_ref, out_ref, rows, turned, mixed):
    _, occupied, local, virtual = in_ref.shape
    targets, _, depth, lanes = out_ref.shape
    tiles = range(virtual // lanes)
    for d1 in range(occupied):
        for t in tiles:
            rows[t, pl.ds(local * d1, local), :] = in_ref[0, d1, :, t * lanes:(t + 1) * lanes]
    for d2 in range(0, local, 2):
        for t in tiles:
            both = [rows[t, pl.ds(d2 + s, occupied, stride=local), :] for s in range(2)]
            turned[pl.ds(t * lanes, lanes), :] = jnp.concatenate(both, axis=0).T
        even = turned[pl.ds(0, virtual // 2, stride=2), :]
        odd = turned[pl.ds(1, virtual // 2, stride=2), :]
        for s in range(2):
            at = slice(s * occupied, (s + 1) * occupied)
            mixed[pl.ds(d2 + s, virtual // 2, stride=local), :] = jnp.concatenate(
                [even[:, at], odd[:, at]], axis=1
            )
    for target in range(targets):
        out_ref[target, 0] = mixed[pl.ds(depth * target, depth), :]


def pack_amplitudes(amplitudes, targets):
    window, occupied, local, virtual = amplitudes.shape
    depth = virtual // targets // 2 * local
    return pl.pallas_call(
        pack_amplitudes_kernel,
        grid=(window,),
        out_shape=jax.ShapeDtypeStruct((targets, window, depth, 2 * occupied), jnp.float32),
        in_specs=[pl.BlockSpec((1, occupied, local, virtual), lambda a: (a, 0, 0, 0))],
        out_specs=pl.BlockSpec((targets, 1, depth, 2 * occupied), lambda a: (0, a, 0, 0)),
        scratch_shapes=[
            pltpu.VMEM((virtual // (2 * occupied), occupied * local, 2 * occupied), jnp.float32),
            pltpu.VMEM((virtual, 2 * occupied), jnp.float32),
            pltpu.VMEM((virtual // 2 * local, 2 * occupied), jnp.float32),
        ],
        compiler_params=pltpu.CompilerParams(vmem_limit_bytes=16 * MIB),
        cost_estimate=pl.CostEstimate(
            flops=0, bytes_accessed=8 * amplitudes.size, transcendentals=0
        ),
    )(amplitudes)


def spin_kernel(in_ref, high_ref, low_ref, block, mixed):
    sources, window, depth, lanes = in_ref.shape
    occupied = lanes // 2
    orbs = sources // 2
    local = occupied // orbs
    for xl in range(2):
        for a in range(window):
            row = (xl * window + a) * occupied // 2
            for c in range(depth // local):
                slot = c % 2
                for orb in range(orbs):
                    block[slot, pl.ds(local * orb, local), :] = in_ref[
                        2 * orb + xl, a, c * local:(c + 1) * local
                    ]
                swapped = block[slot]
                turned = swapped.T
                direct = jnp.concatenate([turned[:occupied], turned[occupied:]], axis=1)
                spin = 2.0 * direct - swapped
                for orb in range(orbs):
                    to = (orb % 2) * occupied // 2 + orb // 2 * local
                    mixed[slot, pl.ds(to, local), :] = spin[local * orb:local * (orb + 1)]
                for core in range(2):
                    rows = mixed[slot, pl.ds(core * occupied // 2, occupied // 2), :]
                    high = rows.astype(jnp.bfloat16)
                    at = (core, slice(row, row + occupied // 2), slice(c * lanes, (c + 1) * lanes))
                    high_ref[at] = high
                    low_ref[at] = (rows - high.astype(jnp.float32)).astype(jnp.bfloat16)


def spin_rows(got):
    sources, window, depth, lanes = got.shape
    occupied = lanes // 2
    local = 2 * occupied // sources
    shape = jax.ShapeDtypeStruct((2, window * occupied, depth // local * lanes), jnp.bfloat16)
    return pl.pallas_call(
        spin_kernel,
        out_shape=(shape, shape),
        in_specs=[VMEM],
        out_specs=(VMEM, VMEM),
        scratch_shapes=[pltpu.VMEM((2, occupied, lanes), jnp.float32)] * 2,
        compiler_params=pltpu.CompilerParams(vmem_limit_bytes=8 * MIB),
        cost_estimate=pl.CostEstimate(flops=0, bytes_accessed=8 * got.size, transcendentals=0),
    )(got)


def product_kernel(count, core_ref, high_ref, low_ref, *refs):
    *in_refs, own_ref, other_ref, left, right, right_high, right_low, sems = refs
    columns_refs, split = in_refs[:count], in_refs[count:]
    xs, width, depth = columns_refs[0].shape
    core = core_ref[0]
    rows = high_ref.shape[1]
    total_count = right_high.shape[0] // (xs * width)
    copies = [
        pltpu.make_async_copy(ref, right.at[r], sems.at[r]) for r, ref in enumerate(columns_refs)
    ]
    ready, at = [], count * xs * width
    for i, ref in enumerate(split):
        to = right_low if i % 2 else right_high
        place = pl.ds(at, ref.shape[0])
        ready.append(pltpu.make_async_copy(ref, to.at[place], sems.at[total_count + 4 + i]))
        at += ref.shape[0] * (i % 2)
    halves = [
        pltpu.make_async_copy(
            ref.at[side], left.at[i, pl.ds(part * rows, rows)], sems.at[total_count + 2 * i + part]
        )
        for i, ref in enumerate((high_ref, low_ref))
        for part, side in enumerate((core, 1 - core))
    ]
    for copy in copies[:2] + halves + copies[2:] + ready:
        copy.start()

    def dot(left, right):
        return lax.dot_general(
            left, right, (((1,), (1,)), ((), ())), preferred_element_type=jnp.float32
        )

    ys, xls, window, local = own_ref.shape[:4]
    group = 4
    for first in range(0, total_count, group):
        if first + group == total_count:
            for copy in ready:
                copy.wait()
        for r in range(first, min(first + group, count)):
            copies[r].wait()
            block = right[r].reshape(xs * width, depth)
            high = block.astype(jnp.bfloat16)
            at = pl.ds(r * xs * width, xs * width)
            right_high[at] = high
            right_low[at] = (block - high.astype(jnp.float32)).astype(jnp.bfloat16)
        if first == 0:
            for copy in halves:
                copy.wait()
        at = pl.ds(first * xs * width, group * xs * width)
        high, low = right_high[at], right_low[at]
        total = dot(left[0], low) + dot(left[1], high) + dot(left[0], high)
        for i, ref in enumerate((own_ref, other_ref)):
            for xl in range(xls):
                for a in range(window):
                    for y in range(ys):
                        start = i * rows + ((xl * window + a) * ys + y) * local
                        ref[y, xl, a, :, first * xs * width:(first + group) * xs * width] = total[
                            start:start + local
                        ]


def product(core, high, low, columns, ready, ys, window, local):
    xs, width, depth = columns[0].shape
    rows = high.shape[1]
    block = xs * len(columns) * width + sum(part.shape[0] for part in ready[::2])
    count = block // (xs * width)
    shape = jax.ShapeDtypeStruct((ys, 2, window, local, block), jnp.float32)
    return pl.pallas_call(
        functools.partial(product_kernel, len(columns)),
        out_shape=(shape, shape),
        in_specs=[pl.BlockSpec(memory_space=pltpu.SMEM)]
        + [pl.BlockSpec(memory_space=pl.ANY)] * (2 + len(columns) + len(ready)),
        out_specs=(VMEM, VMEM),
        scratch_shapes=[
            pltpu.VMEM((2, 2 * rows, depth), jnp.bfloat16),
            pltpu.VMEM((count, xs, width, depth), jnp.float32),
            pltpu.VMEM((block, depth), jnp.bfloat16),
            pltpu.VMEM((block, depth), jnp.bfloat16),
            pltpu.SemaphoreType.DMA((count + 4 + len(ready),)),
        ],
        compiler_params=pltpu.CompilerParams(vmem_limit_bytes=52 * MIB),
        cost_estimate=pl.CostEstimate(
            flops=12 * rows * depth * block, bytes_accessed=8 << 20, transcendentals=0
        ),
    )(core, high, low, *columns, *ready)


def split_kernel(*refs):
    *in_refs, high_ref, low_ref = refs
    xs, width, depth = in_refs[0].shape
    for i, ref in enumerate(in_refs):
        block = ref[...].reshape(xs * width, depth)
        high = block.astype(jnp.bfloat16)
        at = slice(i * xs * width, (i + 1) * xs * width)
        high_ref[at] = high
        low_ref[at] = (block - high.astype(jnp.float32)).astype(jnp.bfloat16)


def split(*blocks):
    xs, width, depth = blocks[0].shape
    shape = jax.ShapeDtypeStruct((len(blocks) * xs * width, depth), jnp.bfloat16)
    return pl.pallas_call(
        split_kernel,
        out_shape=(shape, shape),
        in_specs=[VMEM] * len(blocks),
        out_specs=(VMEM, VMEM),
        compiler_params=pltpu.CompilerParams(vmem_limit_bytes=8 * MIB),
        cost_estimate=pl.CostEstimate(
            flops=28_000_000_000, bytes_accessed=8 * blocks[0].size, transcendentals=0
        ),
    )(*blocks)


ORDER = (1, 3, -1, -3, -4, 0, 2, -2, 4, 5, 6, 7)


def finish_kernel(z_ref, parts_ref, symmetry_ref, out_ref, rows):
    sources, window, local, columns = parts_ref.shape
    zs = 12
    width = columns // zs
    for a in range(window):
        total = parts_ref[0, a]
        for source in range(1, sources):
            total = total + parts_ref[source, a]
        rows[pl.ds(a * local, local), :] = total
    blocks = rows[...]
    blocks = jnp.concatenate(
        [blocks[:, ORDER.index(r) * width:(ORDER.index(r) + 1) * width] for r in range(-4, 8)], axis=1
    )
    turned = pltpu.roll(blocks, lax.rem(z_ref[0] + zs - 4, zs) * width, 1)
    ordered = jnp.concatenate(
        [
            turned[:, z * width + x * 16:z * width + (x + 1) * 16]
            for x in range(width // 16)
            for z in range(zs)
        ],
        axis=1,
    )
    for a in range(window):
        out_ref[a] = jnp.where(
            symmetry_ref[a] == 0, ordered[a * local:(a + 1) * local], jnp.float32(0.0)
        )


def finish(z, parts, symmetry):
    _, window, local, columns = parts.shape
    return pl.pallas_call(
        finish_kernel,
        out_shape=jax.ShapeDtypeStruct((window, local, columns), jnp.float32),
        in_specs=[pl.BlockSpec(memory_space=pltpu.SMEM), VMEM, VMEM],
        out_specs=VMEM,
        scratch_shapes=[pltpu.VMEM((16, columns), jnp.float32)],
        compiler_params=pltpu.CompilerParams(vmem_limit_bytes=8 * MIB),
    )(z, parts, symmetry)


def gather(block, axis, hops, sign):
    size = lax.axis_size(axis)
    pairs = [(i, (i - sign) % size) for i in range(size)]
    blocks = [block]
    for _ in range(hops):
        blocks.append(lax.ppermute(blocks[-1], axis, pairs))
    return blocks[1:]


def body(amplitudes, integrals, a_irrep, b_irrep, occ_irrep):
    window, occupied, local, virtual = amplitudes.shape
    ys = lax.axis_size("y")
    orb = lax.axis_index("y") * 2 + lax.axis_index("core")

    local_occ = lax.dynamic_slice_in_dim(occ_irrep, orb * local, local)
    col_sym = jnp.bitwise_xor(b_irrep[:, None], occ_irrep[None, :]).reshape(-1)
    symmetry = jnp.bitwise_xor(
        jnp.bitwise_xor(a_irrep[:, None, None], local_occ[None, :, None]), col_sym[None, None, :]
    )

    sent = pack_integrals(integrals)
    got = lax.all_to_all(sent, ("xh", "xl"), 0, 0, tiled=True)
    half = lax.axis_size("z") // 2
    ahead = gather(got, "z", half - 1, 1)
    behind = gather(got, "z", half - 1, -1)

    packed = pack_amplitudes(amplitudes, 4 * ys)
    halves = split(got)
    packed, *halves = lax.optimization_barrier((packed, *halves))
    nearby = split(ahead[1], behind[1])
    packed = lax.all_to_all(packed, ("y", "core", "xl"), 0, 0, tiled=True)
    packed, symmetry, *nearby = lax.optimization_barrier((packed, symmetry, *nearby))
    halves += nearby
    high, low = spin_rows(packed)
    last, high, low = lax.optimization_barrier((ahead[-1], high, low))
    ahead += gather(last, "z", 1, 1)

    core = lax.axis_index("core").astype(jnp.int32).reshape(1)
    swap = [(0, 1), (1, 0)]
    early = [ahead[0], ahead[2], behind[0], behind[2], behind[3]]
    late = ahead[3:] + behind[4:]
    own, given = product(core, high, low, early, halves, ys, window, local)
    given, late[2] = lax.optimization_barrier((given, late[2]))
    taken = lax.ppermute(given, "core", swap)
    own_late, given = product(core, high, low, late, [], ys, window, local)
    partial = jnp.concatenate([own + taken, own_late + lax.ppermute(given, "core", swap)], axis=-1)

    partial = partial.reshape(2 * ys, window, local, -1)
    partial = lax.all_to_all(partial, ("y", "xl"), 0, 0, tiled=True)
    z = lax.axis_index("z").astype(jnp.int32).reshape(1)
    return finish(z, partial, symmetry)


def solution(mesh):
    split = Mesh(mesh.devices.reshape(2, 2, 12, 8, 2), ("xh", "xl", "z", "y", "core"))
    pair, orb = ("xh", "xl", "z"), ("y", "core")
    placed = (P(pair, None, orb, None), P(orb, None, pair), P(pair), P(), P())
    return jax.shard_map(
        body, mesh=split, in_specs=placed, out_specs=P(pair, orb, None), check_vma=False
    )
```

```python
import functools

import jax
import jax.numpy as jnp
from jax import lax
from jax.experimental import pallas as pl
from jax.experimental.pallas import tpu as pltpu
from jax.sharding import Mesh, PartitionSpec as P

MIB = 1 << 20
VMEM = pl.BlockSpec(memory_space=pltpu.VMEM)


def pack_integrals_kernel(in_ref, out_ref):
    share, _, occupied = in_ref.shape
    half = share // 2
    for xl in range(2):
        for c in range(0, half, 2):
            first = xl * half + c
            pair = jnp.concatenate([in_ref[first], in_ref[first + 1]], axis=1)
            for xh in range(2):
                out_ref[2 * xh + xl, :, c * occupied:(c + 2) * occupied] = pair


def pack_integrals(integrals):
    share, occupied, width = integrals.shape
    return pl.pallas_call(
        pack_integrals_kernel,
        out_shape=jax.ShapeDtypeStruct((4, width, share // 2 * occupied), jnp.float32),
        in_specs=[VMEM],
        out_specs=VMEM,
    )(integrals.transpose(0, 2, 1))


def pack_amplitudes_kernel(in_ref, out_ref, rows, turned, mixed):
    _, occupied, local, virtual = in_ref.shape
    targets, _, depth, lanes = out_ref.shape
    tiles = range(virtual // lanes)
    for d1 in range(occupied):
        for t in tiles:
            rows[t, pl.ds(local * d1, local), :] = in_ref[0, d1, :, t * lanes:(t + 1) * lanes]
    for d2 in range(0, local, 2):
        for t in tiles:
            both = [rows[t, pl.ds(d2 + s, occupied, stride=local), :] for s in range(2)]
            turned[pl.ds(t * lanes, lanes), :] = jnp.concatenate(both, axis=0).T
        even = turned[pl.ds(0, virtual // 2, stride=2), :]
        odd = turned[pl.ds(1, virtual // 2, stride=2), :]
        for s in range(2):
            at = slice(s * occupied, (s + 1) * occupied)
            mixed[pl.ds(d2 + s, virtual // 2, stride=local), :] = jnp.concatenate(
                [even[:, at], odd[:, at]], axis=1
            )
    for target in range(targets):
        out_ref[target, 0] = mixed[pl.ds(depth * target, depth), :]


def pack_amplitudes(amplitudes, targets):
    window, occupied, local, virtual = amplitudes.shape
    depth = virtual // targets // 2 * local
    return pl.pallas_call(
        pack_amplitudes_kernel,
        grid=(window,),
        out_shape=jax.ShapeDtypeStruct((targets, window, depth, 2 * occupied), jnp.float32),
        in_specs=[pl.BlockSpec((1, occupied, local, virtual), lambda a: (a, 0, 0, 0))],
        out_specs=pl.BlockSpec((targets, 1, depth, 2 * occupied), lambda a: (0, a, 0, 0)),
        scratch_shapes=[
            pltpu.VMEM((virtual // (2 * occupied), occupied * local, 2 * occupied), jnp.float32),
            pltpu.VMEM((virtual, 2 * occupied), jnp.float32),
            pltpu.VMEM((virtual // 2 * local, 2 * occupied), jnp.float32),
        ],
        compiler_params=pltpu.CompilerParams(vmem_limit_bytes=16 * MIB),
        cost_estimate=pl.CostEstimate(
            flops=0, bytes_accessed=8 * amplitudes.size, transcendentals=0
        ),
    )(amplitudes)


def spin_kernel(in_ref, high_ref, low_ref, block, mixed):
    sources, window, depth, lanes = in_ref.shape
    occupied = lanes // 2
    orbs = sources // 2
    local = occupied // orbs
    for xl in range(2):
        for a in range(window):
            row = (xl * window + a) * occupied // 2
            for c in range(depth // local):
                slot = c % 2
                for orb in range(orbs):
                    block[slot, pl.ds(local * orb, local), :] = in_ref[
                        2 * orb + xl, a, c * local:(c + 1) * local
                    ]
                swapped = block[slot]
                turned = swapped.T
                direct = jnp.concatenate([turned[:occupied], turned[occupied:]], axis=1)
                spin = 2.0 * direct - swapped
                for orb in range(orbs):
                    to = (orb % 2) * occupied // 2 + orb // 2 * local
                    mixed[slot, pl.ds(to, local), :] = spin[local * orb:local * (orb + 1)]
                for core in range(2):
                    rows = mixed[slot, pl.ds(core * occupied // 2, occupied // 2), :]
                    high = rows.astype(jnp.bfloat16)
                    at = (core, slice(row, row + occupied // 2), slice(c * lanes, (c + 1) * lanes))
                    high_ref[at] = high
                    low_ref[at] = (rows - high.astype(jnp.float32)).astype(jnp.bfloat16)


def spin_rows(got):
    sources, window, depth, lanes = got.shape
    occupied = lanes // 2
    local = 2 * occupied // sources
    shape = jax.ShapeDtypeStruct((2, window * occupied, depth // local * lanes), jnp.bfloat16)
    return pl.pallas_call(
        spin_kernel,
        out_shape=(shape, shape),
        in_specs=[VMEM],
        out_specs=(VMEM, VMEM),
        scratch_shapes=[pltpu.VMEM((2, occupied, lanes), jnp.float32)] * 2,
        compiler_params=pltpu.CompilerParams(vmem_limit_bytes=53 * MIB),
        cost_estimate=pl.CostEstimate(flops=0, bytes_accessed=8 * got.size, transcendentals=0),
    )(got)


def product_kernel(count, core_ref, high_ref, low_ref, *refs):
    *in_refs, own_ref, other_ref, left, right, right_high, right_low, sems = refs
    columns_refs, split = in_refs[:count], in_refs[count:]
    xs, width, depth = columns_refs[0].shape
    core = core_ref[0]
    rows = high_ref.shape[1]
    total_count = right_high.shape[0] // (xs * width)
    copies = [
        pltpu.make_async_copy(ref, right.at[r], sems.at[r]) for r, ref in enumerate(columns_refs)
    ]
    ready, at = [], count * xs * width
    for i, ref in enumerate(split):
        to = right_low if i % 2 else right_high
        place = pl.ds(at, ref.shape[0])
        ready.append(pltpu.make_async_copy(ref, to.at[place], sems.at[total_count + 4 + i]))
        at += ref.shape[0] * (i % 2)
    halves = [
        pltpu.make_async_copy(
            ref.at[side], left.at[i, pl.ds(part * rows, rows)], sems.at[total_count + 2 * i + part]
        )
        for i, ref in enumerate((high_ref, low_ref))
        for part, side in enumerate((core, 1 - core))
    ]
    for copy in copies[:2] + halves + copies[2:] + ready:
        copy.start()

    def dot(left, right):
        return lax.dot_general(
            left, right, (((1,), (1,)), ((), ())), preferred_element_type=jnp.float32
        )

    ys, xls, window, local = own_ref.shape[:4]
    group = total_count
    for first in range(0, total_count, group):
        if first + group == total_count:
            for copy in ready:
                copy.wait()
        for r in range(first, min(first + group, count)):
            copies[r].wait()
            block = right[r].reshape(xs * width, depth)
            high = block.astype(jnp.bfloat16)
            at = pl.ds(r * xs * width, xs * width)
            right_high[at] = high
            right_low[at] = (block - high.astype(jnp.float32)).astype(jnp.bfloat16)
        if first == 0:
            for copy in halves:
                copy.wait()
        at = pl.ds(first * xs * width, group * xs * width)
        high, low = right_high[at], right_low[at]
        total = dot(left[0], low) + dot(left[1], high) + dot(left[0], high)
        for i, ref in enumerate((own_ref, other_ref)):
            for xl in range(xls):
                for a in range(window):
                    for y in range(ys):
                        start = i * rows + ((xl * window + a) * ys + y) * local
                        ref[y, xl, a, :, first * xs * width:(first + group) * xs * width] = total[
                            start:start + local
                        ]


def product(core, high, low, columns, ready, ys, window, local):
    xs, width, depth = columns[0].shape
    rows = high.shape[1]
    block = xs * len(columns) * width + sum(part.shape[0] for part in ready[::2])
    count = block // (xs * width)
    shape = jax.ShapeDtypeStruct((ys, 2, window, local, block), jnp.float32)
    return pl.pallas_call(
        functools.partial(product_kernel, len(columns)),
        out_shape=(shape, shape),
        in_specs=[pl.BlockSpec(memory_space=pltpu.SMEM)]
        + [pl.BlockSpec(memory_space=pl.ANY)] * (2 + len(columns) + len(ready)),
        out_specs=(VMEM, VMEM),
        scratch_shapes=[
            pltpu.VMEM((2, 2 * rows, depth), jnp.bfloat16),
            pltpu.VMEM((count, xs, width, depth), jnp.float32),
            pltpu.VMEM((block, depth), jnp.bfloat16),
            pltpu.VMEM((block, depth), jnp.bfloat16),
            pltpu.SemaphoreType.DMA((count + 4 + len(ready),)),
        ],
        compiler_params=pltpu.CompilerParams(vmem_limit_bytes=53 * MIB),
        cost_estimate=pl.CostEstimate(
            flops=12 * rows * depth * block, bytes_accessed=8 << 20, transcendentals=0
        ),
    )(core, high, low, *columns, *ready)


def split_kernel(*refs):
    *in_refs, high_ref, low_ref = refs
    xs, width, depth = in_refs[0].shape
    for i, ref in enumerate(in_refs):
        block = ref[...].reshape(xs * width, depth)
        high = block.astype(jnp.bfloat16)
        at = slice(i * xs * width, (i + 1) * xs * width)
        high_ref[at] = high
        low_ref[at] = (block - high.astype(jnp.float32)).astype(jnp.bfloat16)


def split(*blocks):
    xs, width, depth = blocks[0].shape
    shape = jax.ShapeDtypeStruct((len(blocks) * xs * width, depth), jnp.bfloat16)
    return pl.pallas_call(
        split_kernel,
        out_shape=(shape, shape),
        in_specs=[VMEM] * len(blocks),
        out_specs=(VMEM, VMEM),
        compiler_params=pltpu.CompilerParams(vmem_limit_bytes=53 * MIB),
        cost_estimate=pl.CostEstimate(
            flops=22_000_000_000, bytes_accessed=8 * blocks[0].size, transcendentals=0
        ),
    )(*blocks)


ORDER = (1, 3, -1, -3, -4, 0, 2, -2, 4, 5, 6, 7)


def finish_kernel(z_ref, parts_ref, symmetry_ref, out_ref, rows):
    sources, window, local, columns = parts_ref.shape
    zs = 12
    width = columns // zs
    for a in range(window):
        total = parts_ref[0, a]
        for source in range(1, sources):
            total = total + parts_ref[source, a]
        rows[pl.ds(a * local, local), :] = total
    blocks = rows[...]
    blocks = jnp.concatenate(
        [blocks[:, ORDER.index(r) * width:(ORDER.index(r) + 1) * width] for r in range(-4, 8)], axis=1
    )
    turned = pltpu.roll(blocks, lax.rem(z_ref[0] + zs - 4, zs) * width, 1)
    ordered = jnp.concatenate(
        [
            turned[:, z * width + x * 16:z * width + (x + 1) * 16]
            for x in range(width // 16)
            for z in range(zs)
        ],
        axis=1,
    )
    for a in range(window):
        out_ref[a] = jnp.where(
            symmetry_ref[a] == 0, ordered[a * local:(a + 1) * local], jnp.float32(0.0)
        )


def finish(z, parts, symmetry):
    _, window, local, columns = parts.shape
    return pl.pallas_call(
        finish_kernel,
        out_shape=jax.ShapeDtypeStruct((window, local, columns), jnp.float32),
        in_specs=[pl.BlockSpec(memory_space=pltpu.SMEM), VMEM, VMEM],
        out_specs=VMEM,
        scratch_shapes=[pltpu.VMEM((16, columns), jnp.float32)],
        compiler_params=pltpu.CompilerParams(vmem_limit_bytes=53 * MIB),
    )(z, parts, symmetry)


def gather(block, axis, hops, sign):
    size = lax.axis_size(axis)
    pairs = [(i, (i - sign) % size) for i in range(size)]
    blocks = [block]
    for _ in range(hops):
        blocks.append(lax.ppermute(blocks[-1], axis, pairs))
    return blocks[1:]


def body(amplitudes, integrals, a_irrep, b_irrep, occ_irrep):
    window, occupied, local, virtual = amplitudes.shape
    ys = lax.axis_size("y")
    orb = lax.axis_index("y") * 2 + lax.axis_index("core")

    local_occ = lax.dynamic_slice_in_dim(occ_irrep, orb * local, local)
    col_sym = jnp.bitwise_xor(b_irrep[:, None], occ_irrep[None, :]).reshape(-1)
    symmetry = jnp.bitwise_xor(
        jnp.bitwise_xor(a_irrep[:, None, None], local_occ[None, :, None]), col_sym[None, None, :]
    )

    sent = pack_integrals(integrals)
    got = lax.all_to_all(sent, ("xh", "xl"), 0, 0, tiled=True)
    half = lax.axis_size("z") // 2
    ahead = gather(got, "z", half - 1, 1)
    behind = gather(got, "z", half - 1, -1)

    packed = pack_amplitudes(amplitudes, 4 * ys)
    halves = split(got)
    packed, *halves = lax.optimization_barrier((packed, *halves))
    nearby = split(ahead[1], behind[1])
    packed = lax.all_to_all(packed, ("y", "core", "xl"), 0, 0, tiled=True)
    packed, symmetry, *nearby = lax.optimization_barrier((packed, symmetry, *nearby))
    halves += nearby
    high, low = spin_rows(packed)
    ahead += gather(ahead[-1], "z", 1, 1)

    core = lax.axis_index("core").astype(jnp.int32).reshape(1)
    swap = [(0, 1), (1, 0)]
    early = [ahead[0], ahead[2], behind[0], behind[2], behind[3]]
    late = ahead[3:] + behind[4:]
    own, given = product(core, high, low, early, halves, ys, window, local)
    given, late[2] = lax.optimization_barrier((given, late[2]))
    taken = lax.ppermute(given, "core", swap)
    own_late, given = product(core, high, low, late, [], ys, window, local)
    partial = jnp.concatenate([own + taken, own_late + lax.ppermute(given, "core", swap)], axis=-1)

    partial = partial.reshape(2 * ys, window, local, -1)
    partial = lax.all_to_all(partial, ("y", "xl"), 0, 0, tiled=True)
    z = lax.axis_index("z").astype(jnp.int32).reshape(1)
    return finish(z, partial, symmetry)


def solution(mesh):
    split = Mesh(mesh.devices.reshape(2, 2, 12, 8, 2), ("xh", "xl", "z", "y", "core"))
    pair, orb = ("xh", "xl", "z"), ("y", "core")
    placed = (P(pair, None, orb, None), P(orb, None, pair), P(pair), P(), P())
    return jax.shard_map(
        body, mesh=split, in_specs=placed, out_specs=P(pair, orb, None), check_vma=False
    )
```

```python
import functools

import jax
import jax.numpy as jnp
from jax import lax
from jax.experimental import pallas as pl
from jax.experimental.pallas import tpu as pltpu
from jax.sharding import Mesh, PartitionSpec as P

MIB = 1 << 20
VMEM = pl.BlockSpec(memory_space=pltpu.VMEM)


def pack_integrals_kernel(in_ref, out_ref):
    share, _, occupied = in_ref.shape
    half = share // 2
    for xl in range(2):
        for c in range(0, half, 2):
            first = xl * half + c
            pair = jnp.concatenate([in_ref[first], in_ref[first + 1]], axis=1)
            for xh in range(2):
                out_ref[2 * xh + xl, :, c * occupied:(c + 2) * occupied] = pair


def pack_integrals(integrals):
    share, occupied, width = integrals.shape
    return pl.pallas_call(
        pack_integrals_kernel,
        out_shape=jax.ShapeDtypeStruct((4, width, share // 2 * occupied), jnp.float32),
        in_specs=[VMEM],
        out_specs=VMEM,
    )(integrals.transpose(0, 2, 1))


def pack_amplitudes_kernel(in_ref, out_ref, rows, turned, mixed):
    _, occupied, local, virtual = in_ref.shape
    targets, _, depth, lanes = out_ref.shape
    tiles = range(virtual // lanes)
    for d1 in range(occupied):
        for t in tiles:
            rows[t, pl.ds(local * d1, local), :] = in_ref[0, d1, :, t * lanes:(t + 1) * lanes]
    for d2 in range(0, local, 2):
        for t in tiles:
            both = [rows[t, pl.ds(d2 + s, occupied, stride=local), :] for s in range(2)]
            turned[pl.ds(t * lanes, lanes), :] = jnp.concatenate(both, axis=0).T
        even = turned[pl.ds(0, virtual // 2, stride=2), :]
        odd = turned[pl.ds(1, virtual // 2, stride=2), :]
        for s in range(2):
            at = slice(s * occupied, (s + 1) * occupied)
            mixed[pl.ds(d2 + s, virtual // 2, stride=local), :] = jnp.concatenate(
                [even[:, at], odd[:, at]], axis=1
            )
    for target in range(targets):
        out_ref[target, 0] = mixed[pl.ds(depth * target, depth), :]


def pack_amplitudes(amplitudes, targets):
    window, occupied, local, virtual = amplitudes.shape
    depth = virtual // targets // 2 * local
    return pl.pallas_call(
        pack_amplitudes_kernel,
        grid=(window,),
        out_shape=jax.ShapeDtypeStruct((targets, window, depth, 2 * occupied), jnp.float32),
        in_specs=[pl.BlockSpec((1, occupied, local, virtual), lambda a: (a, 0, 0, 0))],
        out_specs=pl.BlockSpec((targets, 1, depth, 2 * occupied), lambda a: (0, a, 0, 0)),
        scratch_shapes=[
            pltpu.VMEM((virtual // (2 * occupied), occupied * local, 2 * occupied), jnp.float32),
            pltpu.VMEM((virtual, 2 * occupied), jnp.float32),
            pltpu.VMEM((virtual // 2 * local, 2 * occupied), jnp.float32),
        ],
        compiler_params=pltpu.CompilerParams(vmem_limit_bytes=16 * MIB),
        cost_estimate=pl.CostEstimate(
            flops=0, bytes_accessed=8 * amplitudes.size, transcendentals=0
        ),
    )(amplitudes)


def spin_kernel(in_ref, high_ref, low_ref, block, mixed):
    sources, window, depth, lanes = in_ref.shape
    occupied = lanes // 2
    orbs = sources // 2
    local = occupied // orbs
    for xl in range(2):
        for a in range(window):
            row = (xl * window + a) * occupied // 2
            for c in range(depth // local):
                slot = c % 2
                for orb in range(orbs):
                    block[slot, pl.ds(local * orb, local), :] = in_ref[
                        2 * orb + xl, a, c * local:(c + 1) * local
                    ]
                swapped = block[slot]
                turned = swapped.T
                direct = jnp.concatenate([turned[:occupied], turned[occupied:]], axis=1)
                spin = 2.0 * direct - swapped
                for orb in range(orbs):
                    to = (orb % 2) * occupied // 2 + orb // 2 * local
                    mixed[slot, pl.ds(to, local), :] = spin[local * orb:local * (orb + 1)]
                for core in range(2):
                    rows = mixed[slot, pl.ds(core * occupied // 2, occupied // 2), :]
                    high = rows.astype(jnp.bfloat16)
                    at = (core, slice(row, row + occupied // 2), slice(c * lanes, (c + 1) * lanes))
                    high_ref[at] = high
                    low_ref[at] = (rows - high.astype(jnp.float32)).astype(jnp.bfloat16)


def spin_rows(got):
    sources, window, depth, lanes = got.shape
    occupied = lanes // 2
    local = 2 * occupied // sources
    shape = jax.ShapeDtypeStruct((2, window * occupied, depth // local * lanes), jnp.bfloat16)
    return pl.pallas_call(
        spin_kernel,
        out_shape=(shape, shape),
        in_specs=[VMEM],
        out_specs=(VMEM, VMEM),
        scratch_shapes=[pltpu.VMEM((2, occupied, lanes), jnp.float32)] * 2,
        compiler_params=pltpu.CompilerParams(vmem_limit_bytes=8 * MIB),
        cost_estimate=pl.CostEstimate(flops=0, bytes_accessed=8 * got.size, transcendentals=0),
    )(got)


def product_kernel(count, core_ref, high_ref, low_ref, *refs):
    *in_refs, own_ref, other_ref, left, right, right_high, right_low, sems = refs
    columns_refs, split = in_refs[:count], in_refs[count:]
    xs, width, depth = columns_refs[0].shape
    core = core_ref[0]
    rows = high_ref.shape[1]
    total_count = right_high.shape[0] // (xs * width)
    copies = [
        pltpu.make_async_copy(ref, right.at[r], sems.at[r]) for r, ref in enumerate(columns_refs)
    ]
    ready, at = [], count * xs * width
    for i, ref in enumerate(split):
        to = right_low if i % 2 else right_high
        place = pl.ds(at, ref.shape[0])
        ready.append(pltpu.make_async_copy(ref, to.at[place], sems.at[total_count + 4 + i]))
        at += ref.shape[0] * (i % 2)
    halves = [
        pltpu.make_async_copy(
            ref.at[side], left.at[i, pl.ds(part * rows, rows)], sems.at[total_count + 2 * i + part]
        )
        for i, ref in enumerate((high_ref, low_ref))
        for part, side in enumerate((core, 1 - core))
    ]
    for copy in copies[:2] + halves + copies[2:] + ready:
        copy.start()

    def dot(left, right):
        return lax.dot_general(
            left, right, (((1,), (1,)), ((), ())), preferred_element_type=jnp.float32
        )

    ys, xls, window, local = own_ref.shape[:4]
    group = total_count
    for first in range(0, total_count, group):
        if first + group == total_count:
            for copy in ready:
                copy.wait()
        for r in range(first, min(first + group, count)):
            copies[r].wait()
            block = right[r].reshape(xs * width, depth)
            high = block.astype(jnp.bfloat16)
            at = pl.ds(r * xs * width, xs * width)
            right_high[at] = high
            right_low[at] = (block - high.astype(jnp.float32)).astype(jnp.bfloat16)
        if first == 0:
            for copy in halves:
                copy.wait()
        at = pl.ds(first * xs * width, group * xs * width)
        high, low = right_high[at], right_low[at]
        total = dot(left[0], low) + dot(left[1], high) + dot(left[0], high)
        for i, ref in enumerate((own_ref, other_ref)):
            for xl in range(xls):
                for a in range(window):
                    for y in range(ys):
                        start = i * rows + ((xl * window + a) * ys + y) * local
                        ref[y, xl, a, :, first * xs * width:(first + group) * xs * width] = total[
                            start:start + local
                        ]


def product(core, high, low, columns, ready, ys, window, local):
    xs, width, depth = columns[0].shape
    rows = high.shape[1]
    block = xs * len(columns) * width + sum(part.shape[0] for part in ready[::2])
    count = block // (xs * width)
    shape = jax.ShapeDtypeStruct((ys, 2, window, local, block), jnp.float32)
    return pl.pallas_call(
        functools.partial(product_kernel, len(columns)),
        out_shape=(shape, shape),
        in_specs=[pl.BlockSpec(memory_space=pltpu.SMEM)]
        + [pl.BlockSpec(memory_space=pl.ANY)] * (2 + len(columns) + len(ready)),
        out_specs=(VMEM, VMEM),
        scratch_shapes=[
            pltpu.VMEM((2, 2 * rows, depth), jnp.bfloat16),
            pltpu.VMEM((count, xs, width, depth), jnp.float32),
            pltpu.VMEM((block, depth), jnp.bfloat16),
            pltpu.VMEM((block, depth), jnp.bfloat16),
            pltpu.SemaphoreType.DMA((count + 4 + len(ready),)),
        ],
        compiler_params=pltpu.CompilerParams(vmem_limit_bytes=53 * MIB),
        cost_estimate=pl.CostEstimate(
            flops=12 * rows * depth * block, bytes_accessed=8 << 20, transcendentals=0
        ),
    )(core, high, low, *columns, *ready)


def split_kernel(*refs):
    *in_refs, high_ref, low_ref = refs
    xs, width, depth = in_refs[0].shape
    for i, ref in enumerate(in_refs):
        block = ref[...].reshape(xs * width, depth)
        high = block.astype(jnp.bfloat16)
        at = slice(i * xs * width, (i + 1) * xs * width)
        high_ref[at] = high
        low_ref[at] = (block - high.astype(jnp.float32)).astype(jnp.bfloat16)


def split(*blocks):
    xs, width, depth = blocks[0].shape
    shape = jax.ShapeDtypeStruct((len(blocks) * xs * width, depth), jnp.bfloat16)
    return pl.pallas_call(
        split_kernel,
        out_shape=(shape, shape),
        in_specs=[VMEM] * len(blocks),
        out_specs=(VMEM, VMEM),
        compiler_params=pltpu.CompilerParams(vmem_limit_bytes=8 * MIB),
        cost_estimate=pl.CostEstimate(
            flops=26_000_000_000, bytes_accessed=8 * blocks[0].size, transcendentals=0
        ),
    )(*blocks)


ORDER = (1, 3, -1, -3, -4, 0, 2, -2, 4, 5, 6, 7)


def finish_kernel(z_ref, parts_ref, symmetry_ref, out_ref, rows):
    sources, window, local, columns = parts_ref.shape
    zs = 12
    width = columns // zs
    for a in range(window):
        total = parts_ref[0, a]
        for source in range(1, sources):
            total = total + parts_ref[source, a]
        rows[pl.ds(a * local, local), :] = total
    blocks = rows[...]
    blocks = jnp.concatenate(
        [blocks[:, ORDER.index(r) * width:(ORDER.index(r) + 1) * width] for r in range(-4, 8)], axis=1
    )
    turned = pltpu.roll(blocks, lax.rem(z_ref[0] + zs - 4, zs) * width, 1)
    ordered = jnp.concatenate(
        [
            turned[:, z * width + x * 16:z * width + (x + 1) * 16]
            for x in range(width // 16)
            for z in range(zs)
        ],
        axis=1,
    )
    for a in range(window):
        out_ref[a] = jnp.where(
            symmetry_ref[a] == 0, ordered[a * local:(a + 1) * local], jnp.float32(0.0)
        )


def finish(z, parts, symmetry):
    _, window, local, columns = parts.shape
    return pl.pallas_call(
        finish_kernel,
        out_shape=jax.ShapeDtypeStruct((window, local, columns), jnp.float32),
        in_specs=[pl.BlockSpec(memory_space=pltpu.SMEM), VMEM, VMEM],
        out_specs=VMEM,
        scratch_shapes=[pltpu.VMEM((16, columns), jnp.float32)],
        compiler_params=pltpu.CompilerParams(vmem_limit_bytes=8 * MIB),
    )(z, parts, symmetry)


def gather(block, axis, hops, sign):
    size = lax.axis_size(axis)
    pairs = [(i, (i - sign) % size) for i in range(size)]
    blocks = [block]
    for _ in range(hops):
        blocks.append(lax.ppermute(blocks[-1], axis, pairs))
    return blocks[1:]


def body(amplitudes, integrals, a_irrep, b_irrep, occ_irrep):
    window, occupied, local, virtual = amplitudes.shape
    ys = lax.axis_size("y")
    orb = lax.axis_index("y") * 2 + lax.axis_index("core")

    local_occ = lax.dynamic_slice_in_dim(occ_irrep, orb * local, local)
    col_sym = jnp.bitwise_xor(b_irrep[:, None], occ_irrep[None, :]).reshape(-1)
    symmetry = jnp.bitwise_xor(
        jnp.bitwise_xor(a_irrep[:, None, None], local_occ[None, :, None]), col_sym[None, None, :]
    )

    sent = pack_integrals(integrals)
    got = lax.all_to_all(sent, ("xh", "xl"), 0, 0, tiled=True)
    half = lax.axis_size("z") // 2
    ahead = gather(got, "z", half - 1, 1)
    behind = gather(got, "z", 2, -1)
    nearby = split(ahead[1], behind[1])
    last, *nearby = lax.optimization_barrier((behind[1], *nearby))
    behind += gather(last, "z", half - 3, -1)

    packed = pack_amplitudes(amplitudes, 4 * ys)
    halves = split(got)
    packed, *halves = lax.optimization_barrier((packed, *halves))
    packed = lax.all_to_all(packed, ("y", "core", "xl"), 0, 0, tiled=True)
    packed, symmetry = lax.optimization_barrier((packed, symmetry))
    halves += nearby
    high, low = spin_rows(packed)
    ahead += gather(ahead[-1], "z", 1, 1)

    core = lax.axis_index("core").astype(jnp.int32).reshape(1)
    swap = [(0, 1), (1, 0)]
    early = [ahead[0], ahead[2], behind[0], behind[2], behind[3]]
    late = ahead[3:] + behind[4:]
    own, given = product(core, high, low, early, halves, ys, window, local)
    given, late[2] = lax.optimization_barrier((given, late[2]))
    taken = lax.ppermute(given, "core", swap)
    own_late, given = product(core, high, low, late, [], ys, window, local)
    partial = jnp.concatenate([own + taken, own_late + lax.ppermute(given, "core", swap)], axis=-1)

    partial = partial.reshape(2 * ys, window, local, -1)
    partial = lax.all_to_all(partial, ("y", "xl"), 0, 0, tiled=True)
    z = lax.axis_index("z").astype(jnp.int32).reshape(1)
    return finish(z, partial, symmetry)


def solution(mesh):
    split = Mesh(mesh.devices.reshape(2, 2, 12, 8, 2), ("xh", "xl", "z", "y", "core"))
    pair, orb = ("xh", "xl", "z"), ("y", "core")
    placed = (P(pair, None, orb, None), P(orb, None, pair), P(pair), P(), P())
    return jax.shard_map(
        body, mesh=split, in_specs=placed, out_specs=P(pair, orb, None), check_vma=False
    )
```

```python
import functools

import jax
import jax.numpy as jnp
from jax import lax
from jax.experimental import pallas as pl
from jax.experimental.pallas import tpu as pltpu
from jax.sharding import Mesh, PartitionSpec as P

MIB = 1 << 20
VMEM = pl.BlockSpec(memory_space=pltpu.VMEM)


def pack_integrals_kernel(in_ref, out_ref):
    share, _, occupied = in_ref.shape
    half = share // 2
    for xl in range(2):
        for c in range(0, half, 2):
            first = xl * half + c
            pair = jnp.concatenate([in_ref[first], in_ref[first + 1]], axis=1)
            for xh in range(2):
                out_ref[2 * xh + xl, :, c * occupied:(c + 2) * occupied] = pair


def pack_integrals(integrals):
    share, occupied, width = integrals.shape
    return pl.pallas_call(
        pack_integrals_kernel,
        out_shape=jax.ShapeDtypeStruct((4, width, share // 2 * occupied), jnp.float32),
        in_specs=[VMEM],
        out_specs=VMEM,
    )(integrals.transpose(0, 2, 1))


def pack_amplitudes_kernel(in_ref, out_ref, rows, turned, mixed):
    _, occupied, local, virtual = in_ref.shape
    targets, _, depth, lanes = out_ref.shape
    tiles = range(virtual // lanes)
    for d1 in range(occupied):
        for t in tiles:
            rows[t, pl.ds(local * d1, local), :] = in_ref[0, d1, :, t * lanes:(t + 1) * lanes]
    for d2 in range(0, local, 2):
        for t in tiles:
            both = [rows[t, pl.ds(d2 + s, occupied, stride=local), :] for s in range(2)]
            turned[pl.ds(t * lanes, lanes), :] = jnp.concatenate(both, axis=0).T
        even = turned[pl.ds(0, virtual // 2, stride=2), :]
        odd = turned[pl.ds(1, virtual // 2, stride=2), :]
        for s in range(2):
            at = slice(s * occupied, (s + 1) * occupied)
            mixed[pl.ds(d2 + s, virtual // 2, stride=local), :] = jnp.concatenate(
                [even[:, at], odd[:, at]], axis=1
            )
    for target in range(targets):
        out_ref[target, 0] = mixed[pl.ds(depth * target, depth), :]


def pack_amplitudes(amplitudes, targets):
    window, occupied, local, virtual = amplitudes.shape
    depth = virtual // targets // 2 * local
    return pl.pallas_call(
        pack_amplitudes_kernel,
        grid=(window,),
        out_shape=jax.ShapeDtypeStruct((targets, window, depth, 2 * occupied), jnp.float32),
        in_specs=[pl.BlockSpec((1, occupied, local, virtual), lambda a: (a, 0, 0, 0))],
        out_specs=pl.BlockSpec((targets, 1, depth, 2 * occupied), lambda a: (0, a, 0, 0)),
        scratch_shapes=[
            pltpu.VMEM((virtual // (2 * occupied), occupied * local, 2 * occupied), jnp.float32),
            pltpu.VMEM((virtual, 2 * occupied), jnp.float32),
            pltpu.VMEM((virtual // 2 * local, 2 * occupied), jnp.float32),
        ],
        compiler_params=pltpu.CompilerParams(vmem_limit_bytes=16 * MIB),
        cost_estimate=pl.CostEstimate(
            flops=0, bytes_accessed=8 * amplitudes.size, transcendentals=0
        ),
    )(amplitudes)


def spin_kernel(in_ref, high_ref, low_ref, block, mixed):
    sources, window, depth, lanes = in_ref.shape
    occupied = lanes // 2
    orbs = sources // 2
    local = occupied // orbs
    for xl in range(2):
        for a in range(window):
            row = (xl * window + a) * occupied // 2
            for c in range(depth // local):
                slot = c % 2
                for orb in range(orbs):
                    block[slot, pl.ds(local * orb, local), :] = in_ref[
                        2 * orb + xl, a, c * local:(c + 1) * local
                    ]
                swapped = block[slot]
                turned = swapped.T
                direct = jnp.concatenate([turned[:occupied], turned[occupied:]], axis=1)
                spin = 2.0 * direct - swapped
                for orb in range(orbs):
                    to = (orb % 2) * occupied // 2 + orb // 2 * local
                    mixed[slot, pl.ds(to, local), :] = spin[local * orb:local * (orb + 1)]
                for core in range(2):
                    rows = mixed[slot, pl.ds(core * occupied // 2, occupied // 2), :]
                    high = rows.astype(jnp.bfloat16)
                    at = (core, slice(row, row + occupied // 2), slice(c * lanes, (c + 1) * lanes))
                    high_ref[at] = high
                    low_ref[at] = (rows - high.astype(jnp.float32)).astype(jnp.bfloat16)


def spin_rows(got):
    sources, window, depth, lanes = got.shape
    occupied = lanes // 2
    local = 2 * occupied // sources
    shape = jax.ShapeDtypeStruct((2, window * occupied, depth // local * lanes), jnp.bfloat16)
    return pl.pallas_call(
        spin_kernel,
        out_shape=(shape, shape),
        in_specs=[VMEM],
        out_specs=(VMEM, VMEM),
        scratch_shapes=[pltpu.VMEM((2, occupied, lanes), jnp.float32)] * 2,
        compiler_params=pltpu.CompilerParams(vmem_limit_bytes=8 * MIB),
        cost_estimate=pl.CostEstimate(flops=0, bytes_accessed=8 * got.size, transcendentals=0),
    )(got)


def product_kernel(count, core_ref, high_ref, low_ref, *refs):
    *in_refs, own_ref, other_ref, left, right, right_high, right_low, sems = refs
    columns_refs, split = in_refs[:count], in_refs[count:]
    xs, width, depth = columns_refs[0].shape
    core = core_ref[0]
    rows = high_ref.shape[1]
    total_count = right_high.shape[0] // (xs * width)
    copies = [
        pltpu.make_async_copy(ref, right.at[r], sems.at[r]) for r, ref in enumerate(columns_refs)
    ]
    ready, at = [], count * xs * width
    for i, ref in enumerate(split):
        to = right_low if i % 2 else right_high
        place = pl.ds(at, ref.shape[0])
        ready.append(pltpu.make_async_copy(ref, to.at[place], sems.at[total_count + 4 + i]))
        at += ref.shape[0] * (i % 2)
    halves = [
        pltpu.make_async_copy(
            ref.at[side], left.at[i, pl.ds(part * rows, rows)], sems.at[total_count + 2 * i + part]
        )
        for i, ref in enumerate((high_ref, low_ref))
        for part, side in enumerate((core, 1 - core))
    ]
    for copy in copies[:2] + halves + copies[2:] + ready:
        copy.start()

    def dot(left, right):
        return lax.dot_general(
            left, right, (((1,), (1,)), ((), ())), preferred_element_type=jnp.float32
        )

    ys, xls, window, local = own_ref.shape[:4]
    group = total_count
    for first in range(0, total_count, group):
        if first + group == total_count:
            for copy in ready:
                copy.wait()
        for r in range(first, min(first + group, count)):
            copies[r].wait()
            block = right[r].reshape(xs * width, depth)
            high = block.astype(jnp.bfloat16)
            at = pl.ds(r * xs * width, xs * width)
            right_high[at] = high
            right_low[at] = (block - high.astype(jnp.float32)).astype(jnp.bfloat16)
        if first == 0:
            for copy in halves:
                copy.wait()
        at = pl.ds(first * xs * width, group * xs * width)
        high, low = right_high[at], right_low[at]
        total = dot(left[0], low) + dot(left[1], high) + dot(left[0], high)
        for i, ref in enumerate((own_ref, other_ref)):
            for xl in range(xls):
                for a in range(window):
                    for y in range(ys):
                        start = i * rows + ((xl * window + a) * ys + y) * local
                        ref[y, xl, a, :, first * xs * width:(first + group) * xs * width] = total[
                            start:start + local
                        ]


def product(core, high, low, columns, ready, ys, window, local):
    xs, width, depth = columns[0].shape
    rows = high.shape[1]
    block = xs * len(columns) * width + sum(part.shape[0] for part in ready[::2])
    count = block // (xs * width)
    shape = jax.ShapeDtypeStruct((ys, 2, window, local, block), jnp.float32)
    return pl.pallas_call(
        functools.partial(product_kernel, len(columns)),
        out_shape=(shape, shape),
        in_specs=[pl.BlockSpec(memory_space=pltpu.SMEM)]
        + [pl.BlockSpec(memory_space=pl.ANY)] * (2 + len(columns) + len(ready)),
        out_specs=(VMEM, VMEM),
        scratch_shapes=[
            pltpu.VMEM((2, 2 * rows, depth), jnp.bfloat16),
            pltpu.VMEM((count, xs, width, depth), jnp.float32),
            pltpu.VMEM((block, depth), jnp.bfloat16),
            pltpu.VMEM((block, depth), jnp.bfloat16),
            pltpu.SemaphoreType.DMA((count + 4 + len(ready),)),
        ],
        compiler_params=pltpu.CompilerParams(vmem_limit_bytes=53 * MIB),
        cost_estimate=pl.CostEstimate(
            flops=12 * rows * depth * block, bytes_accessed=8 << 20, transcendentals=0
        ),
    )(core, high, low, *columns, *ready)


def split_kernel(*refs):
    *in_refs, high_ref, low_ref = refs
    xs, width, depth = in_refs[0].shape
    for i, ref in enumerate(in_refs):
        block = ref[...].reshape(xs * width, depth)
        high = block.astype(jnp.bfloat16)
        at = slice(i * xs * width, (i + 1) * xs * width)
        high_ref[at] = high
        low_ref[at] = (block - high.astype(jnp.float32)).astype(jnp.bfloat16)


def split(*blocks):
    xs, width, depth = blocks[0].shape
    shape = jax.ShapeDtypeStruct((len(blocks) * xs * width, depth), jnp.bfloat16)
    return pl.pallas_call(
        split_kernel,
        out_shape=(shape, shape),
        in_specs=[VMEM] * len(blocks),
        out_specs=(VMEM, VMEM),
        compiler_params=pltpu.CompilerParams(vmem_limit_bytes=8 * MIB),
        cost_estimate=pl.CostEstimate(
            flops=26_000_000_000, bytes_accessed=8 * blocks[0].size, transcendentals=0
        ),
    )(*blocks)


ORDER = (1, 3, -1, -3, -4, 0, 2, -2, 4, 5, 6, 7)


def finish_kernel(z_ref, parts_ref, symmetry_ref, out_ref, rows):
    sources, window, local, columns = parts_ref.shape
    zs = 12
    width = columns // zs
    for a in range(window):
        total = parts_ref[0, a]
        for source in range(1, sources):
            total = total + parts_ref[source, a]
        rows[pl.ds(a * local, local), :] = total
    blocks = rows[...]
    blocks = jnp.concatenate(
        [blocks[:, ORDER.index(r) * width:(ORDER.index(r) + 1) * width] for r in range(-4, 8)], axis=1
    )
    turned = pltpu.roll(blocks, lax.rem(z_ref[0] + zs - 4, zs) * width, 1)
    ordered = jnp.concatenate(
        [
            turned[:, z * width + x * 16:z * width + (x + 1) * 16]
            for x in range(width // 16)
            for z in range(zs)
        ],
        axis=1,
    )
    for a in range(window):
        out_ref[a] = jnp.where(
            symmetry_ref[a] == 0, ordered[a * local:(a + 1) * local], jnp.float32(0.0)
        )


def finish(z, parts, symmetry):
    _, window, local, columns = parts.shape
    return pl.pallas_call(
        finish_kernel,
        out_shape=jax.ShapeDtypeStruct((window, local, columns), jnp.float32),
        in_specs=[pl.BlockSpec(memory_space=pltpu.SMEM), VMEM, VMEM],
        out_specs=VMEM,
        scratch_shapes=[pltpu.VMEM((16, columns), jnp.float32)],
        compiler_params=pltpu.CompilerParams(vmem_limit_bytes=8 * MIB),
    )(z, parts, symmetry)


def gather(block, axis, hops, sign):
    size = lax.axis_size(axis)
    pairs = [(i, (i - sign) % size) for i in range(size)]
    blocks = [block]
    for _ in range(hops):
        blocks.append(lax.ppermute(blocks[-1], axis, pairs))
    return blocks[1:]


def body(amplitudes, integrals, a_irrep, b_irrep, occ_irrep):
    window, occupied, local, virtual = amplitudes.shape
    ys = lax.axis_size("y")
    orb = lax.axis_index("y") * 2 + lax.axis_index("core")

    local_occ = lax.dynamic_slice_in_dim(occ_irrep, orb * local, local)
    col_sym = jnp.bitwise_xor(b_irrep[:, None], occ_irrep[None, :]).reshape(-1)
    symmetry = jnp.bitwise_xor(
        jnp.bitwise_xor(a_irrep[:, None, None], local_occ[None, :, None]), col_sym[None, None, :]
    )

    sent = pack_integrals(integrals)
    got = lax.all_to_all(sent, ("xh", "xl"), 0, 0, tiled=True)
    half = lax.axis_size("z") // 2
    ahead = gather(got, "z", half - 1, 1)
    behind = gather(got, "z", 2, -1)
    nearby = split(ahead[1], behind[1])
    last, *nearby = lax.optimization_barrier((behind[1], *nearby))
    behind += gather(last, "z", half - 3, -1)

    packed = pack_amplitudes(amplitudes, 4 * ys)
    halves = split(got)
    packed, *halves = lax.optimization_barrier((packed, *halves))
    packed = lax.all_to_all(packed, ("y", "core", "xl"), 0, 0, tiled=True)
    packed, symmetry = lax.optimization_barrier((packed, symmetry))
    halves += nearby
    high, low = spin_rows(packed)
    ahead += gather(ahead[-1], "z", 1, 1)

    core = lax.axis_index("core").astype(jnp.int32).reshape(1)
    swap = [(0, 1), (1, 0)]
    early = [ahead[0], ahead[2], behind[0], behind[2], behind[3]]
    late = ahead[3:] + behind[4:]
    own, given = product(core, high, low, early, halves, ys, window, local)
    given, late[2] = lax.optimization_barrier((given, late[2]))
    own_late, given_late = product(core, high, low, late, [], ys, window, local)
    given, given_late = lax.optimization_barrier((given, given_late))
    taken, taken_late = (lax.ppermute(part, "core", swap) for part in (given, given_late))
    partial = jnp.concatenate([own + taken, own_late + taken_late], axis=-1)

    partial = partial.reshape(2 * ys, window, local, -1)
    partial = lax.all_to_all(partial, ("y", "xl"), 0, 0, tiled=True)
    z = lax.axis_index("z").astype(jnp.int32).reshape(1)
    return finish(z, partial, symmetry)


def solution(mesh):
    split = Mesh(mesh.devices.reshape(2, 2, 12, 8, 2), ("xh", "xl", "z", "y", "core"))
    pair, orb = ("xh", "xl", "z"), ("y", "core")
    placed = (P(pair, None, orb, None), P(orb, None, pair), P(pair), P(), P())
    return jax.shard_map(
        body, mesh=split, in_specs=placed, out_specs=P(pair, orb, None), check_vma=False
    )
```
